32 devices in a mesh: groups: 2 (over y), expert: 8 (over z, x), dp: 2 (over core).
Axes of the slice: x: 2, y: 2, z: 4, core: 2. Of those that a mesh axis runs over, the one named last changes fastest.
Arguments:
- out_grad: bfloat16 [4096, 1280], P(('groups', 'expert', 'dp')), parts along dimension 0, may hold values from -6 to 6
- gates: bfloat16 [4096, 6], P(('groups', 'expert', 'dp')), parts along dimension 0, may hold values from 0.099609375 to 1
- routes: int32 [4096, 6], P(('groups', 'expert', 'dp')), parts along dimension 0, may hold values from 0 to 63, all different within a row; in each aligned block of 128 rows (0 to 127, 128 to 255, ...) at most 14 rows name the same one
- tile_slot: int32 [4096], P(('groups', 'expert', 'dp')), parts along dimension 0, may hold values from -1 to 127, as said below
- w_in: bfloat16 [64, 1280, 768], P('expert', 'dp'), may hold values from -0.15625 to 0.15625
- w_out: bfloat16 [64, 768, 1280], P('expert', None, 'dp'), may hold values from -0.21875 to 0.21875
- expert_pre: bfloat16 [256, 8, 14, 768], P(('groups', 'expert', 'dp')), parts along dimension 0, may hold values from -6 to 6
- adapter_pre: bfloat16 [2048, 1280], P(('groups', 'expert', 'dp')), parts along dimension 0, may hold values from -6 to 6
- w_adapt: bfloat16 [2304, 1280], P(('expert', 'dp')), may hold values from -0.125 to 0.125
Outputs:
- token_grads: bfloat16 [4096, 1280], P(('groups', 'expert', 'dp')), parts along dimension 0
- patch_grads: float32 [512, 9216], P(('groups', 'expert', 'dp')), parts along dimension 0
The draws below stay inside these ranges and needn't reach their ends.
There are 2 independent parts, one for each index of `groups`. The reference program is written for one: setup_inputs(seed, part) draws one part's arguments, and reference() takes and returns one part's arrays. A program takes and returns all parts, laid end to end along the dimension named above; an argument that names none is the same for every part. Nothing has to cross between parts.
Inputs may be any that keep to these rules, and one draw needn't show every extreme that they name: `routes`: in each aligned block of 128 rows (the tokens of one device) no expert is named by more than 14 rows, a bound that some block reaches. `tile_slot`: -1 marks a text token. In each aligned block of 256 tokens every value 0 to 127 appears exactly once; value v belongs to slot v mod 64 of the (v div 64)-th device of the block.
All inputs are finite; a program needn't handle non-finite values.
Results may differ from the reference program's by a relative error of at most 0.0064.
Values may be sent and summed in bfloat16 or wider, within the bound.
A program may use at most 128 MiB of HBM per device.

```python
import math
import jax
import jax.numpy as jnp
import numpy as np
from jax import lax

D = 1280
FW = 768
EXPERTS = 64
TOP = 6
SIGW = 576
TILE_R = 8
TOK_DEV = 128
EXPERT_DEVS = 8
CORE_DEVS = 2
PARTDEV = 16
EXP_IDX = 8
GRP = 8
SLOTS = 64
FWP = 768
MOST = 14
TOKENS = 2048
HROWS = 128
VIS_DEV = 64
VIS_PAIR = 128
PAIR_TOK = 256
TILE_C = 8


def draw_tile_slot(key, part):
    key = jax.random.fold_in(key, 17)
    block_keys = jax.random.split(key, TOKENS // PAIR_TOK)

    def one_block(block_key):
        order = jax.random.permutation(block_key, PAIR_TOK).astype(jnp.int32)
        filled = jnp.full((PAIR_TOK,), -1, jnp.int32)
        return filled.at[order[:VIS_PAIR]].set(jnp.arange(VIS_PAIR, dtype=jnp.int32))
    return jax.vmap(one_block)(block_keys).reshape(TOKENS)


def level_of(key, dims, shards, low, top_value):
    def one(dim, shards_of):
        draws = jax.random.uniform(jax.random.fold_in(jax.random.fold_in(key, 6), dim), (shards_of,), jnp.float32, low / len(shards), top_value / len(shards))
        return jnp.repeat(jnp.exp(draws), dims[dim] // shards_of).reshape((-1,) + (1,) * (len(dims) - dim - 1))

    loudness = one(*shards[0])
    for cut in shards[1:]:
        loudness = loudness * one(*cut)
    return loudness


def shared_out(stream_key, own, number, rows, number_of, top, bound, slope):
    order = jax.random.permutation(stream_key, number_of)
    heavy_load, common = load_shares(number_of, rows * top, bound, slope, True), load_shares(number_of, rows * top, bound, slope, False)
    places = jnp.arange(number_of)

    def named(lengths, offset_by):
        used = int((lengths > 0).sum())
        fixed = max(1, used // 4)
        moved = fixed + (places - fixed + offset_by * (used - fixed)) % max(1, number_of - fixed)
        return jnp.zeros((number_of,), jnp.int32).at[order[jnp.where(places < fixed, places, moved)]].set(jnp.asarray(lengths, jnp.int32))

    lengths = jnp.where(number % 4 == 0, named(heavy_load, number // 4), named(common, number - number // 4 - 1))
    mixed = jax.random.permutation(jax.random.fold_in(own, 3), number_of)
    giver, sink = mixed[0:number_of // 2 * 2:2], mixed[1:number_of // 2 * 2:2]
    margin = jnp.minimum(lengths[giver] - 1, bound - lengths[sink]) // 2
    margin = jnp.where((giver == order[0]) | (sink == order[0]) | (lengths[sink] == 0), 0, jnp.maximum(margin, 0))
    moved = jax.random.randint(jax.random.fold_in(own, 4), (number_of // 2,), 0, 1 << 20) % (margin + 1)
    lengths = lengths.at[giver].add(-moved).at[sink].add(moved)
    members = jnp.searchsorted(jnp.cumsum(lengths), jnp.arange(rows * top), side="right").astype(jnp.int32)
    grid = members.reshape(top, rows).T
    grid = grid[jax.random.permutation(jax.random.fold_in(own, 1), rows)]
    offset_by = jax.random.randint(jax.random.fold_in(own, 2), (rows, 1), 0, top)
    return jnp.take_along_axis(grid, (jnp.arange(top)[None, :] + offset_by) % top, axis=1)


def load_shares(amount, total, most, skew, full):
    portions = [(1 << 20) // math.isqrt(grade ** skew) + 1 for grade in range(1, amount + 1)]
    largest = most if full else min(most, max(-(-total // amount), total * portions[0] // sum(portions)))
    least = 1 if total - largest >= amount - 1 else 0
    given, surplus = [largest] + [least] * (amount - 1), total - largest - least * (amount - 1)
    while surplus > 0:
        movable = [i for i in range(1, amount) if given[i] < largest] or [i for i in range(1, amount) if given[i] < most]
        whole, budget = sum([portions[i] for i in movable]), surplus
        for i in movable:
            more = min(most - given[i], max(1, budget * portions[i] // whole), surplus)
            given[i] = given[i] + more
            surplus = surplus - more
    return np.array(given)


def centred(rng, extent, scale, most, pieces=(), kind=jnp.bfloat16):
    values = jax.random.normal(rng, extent, jnp.float32) * scale
    if len(pieces) > 0:
        values = level_of(rng, extent, pieces, -0.22, 0.18) * values
    return jnp.clip(values, min=-most, max=most).astype(kind)


def setup_inputs(seed: int = 0, part: int = 0) -> dict:
    seeds = jax.random.split(jax.random.key(seed), 10)
    part_keys = jax.random.split(jax.random.fold_in(seeds[9], part), 10)
    out_grad = centred(part_keys[0], (TOKENS, D), 1.0, 6.0, ((0, 16),))
    gates = jnp.clip(0.099609375 + 0.9003906 * jax.random.uniform(part_keys[1], (TOKENS, TOP), jnp.float32) ** level_of(part_keys[1], (TOKENS, TOP), ((0, 16),), -0.2, 0.2), 0.099609375, 1.0).astype(jnp.bfloat16)
    routes_keys = jax.random.split(jax.random.fold_in(part_keys[2], 1), TOKENS // TOK_DEV)
    routes_turns = jax.random.permutation(jax.random.fold_in(part_keys[2], 3), TOKENS // TOK_DEV)
    routes = jax.vmap(lambda own, number: shared_out(jax.random.fold_in(part_keys[2], 2), own, number, TOK_DEV, EXPERTS, TOP, MOST, 2))(routes_keys, routes_turns).reshape((TOKENS, TOP))
    tile_slot = draw_tile_slot(jax.random.fold_in(jax.random.fold_in(seeds[9], part), 71), part)
    w_in = centred(seeds[4], (SLOTS, D, FWP), D ** -0.5, 0.15625, ((0, 8), (1, 2)))
    w_out = centred(seeds[5], (SLOTS, FWP, D), FW ** -0.5, 0.21875, ((0, 8), (2, 2)))
    expert_pre = centred(part_keys[6], (HROWS, EXP_IDX, MOST, FWP), 1.0, 6.0, ((0, 16),))
    adapter_pre = centred(part_keys[7], (PARTDEV * VIS_DEV, D), 1.0, 6.0, ((0, 16),))
    w_adapt = centred(seeds[8], (4 * SIGW, D), (4 * SIGW) ** -0.5, 0.125, ((0, 16),))
    return dict(out_grad=out_grad, gates=gates, routes=routes, tile_slot=tile_slot, w_in=w_in, w_out=w_out, expert_pre=expert_pre, adapter_pre=adapter_pre, w_adapt=w_adapt)


def silu_slope(value):
    sigma = jax.nn.sigmoid(value)
    return sigma * (1.0 + value * (1.0 - sigma))


def gelu_slope(value):
    normal_cdf = 0.5 * (1.0 + lax.erf(value * 0.7071067811865476))
    return normal_cdf + value * jnp.exp(-0.5 * value * value) * 0.3989422804014327


def reference(out_grad, gates, routes, tile_slot, w_in, w_out, expert_pre, adapter_pre, w_adapt):
    block_routes = routes.reshape(PARTDEV, TOK_DEV * TOP)
    expert_hot = (block_routes[:, :, None] == jnp.arange(EXPERTS, dtype=jnp.int32)[None, None, :]).astype(jnp.int32)
    earlier = jnp.cumsum(expert_hot, axis=1) - expert_hot
    row_rank = jnp.sum(earlier * expert_hot, axis=2).reshape(-1).astype(jnp.int32)
    routes_flat = routes.reshape(-1).astype(jnp.int32)
    row_index = jnp.arange(TOKENS * TOP, dtype=jnp.int32)
    token_of = row_index // TOP
    source = token_of // TOK_DEV
    axis_pos = source // CORE_DEVS
    core_pos = source % CORE_DEVS
    local_expert = routes_flat % EXP_IDX
    gate_flat = gates.reshape(-1).astype(jnp.float32)
    capacity_all = PARTDEV * MOST

    def one_piece(running, slot):
        piece = slot // EXPERTS
        expert = slot % EXPERTS
        chosen = routes_flat == expert
        count = jnp.sum(chosen.astype(jnp.int32))
        picked = jnp.nonzero(chosen, size=capacity_all, fill_value=0)[0].astype(jnp.int32)
        valid = jnp.arange(capacity_all, dtype=jnp.int32) < count
        tokens_picked = token_of[picked]
        rows_grad = out_grad[tokens_picked]
        holder = expert // EXP_IDX + GRP * piece
        pre_index = (holder * CORE_DEVS + core_pos[picked]) * EXPERT_DEVS + axis_pos[picked]
        saved = expert_pre[pre_index, local_expert[picked], row_rank[picked]].astype(jnp.float32)
        hidden = jnp.dot(rows_grad, w_out[slot].T, preferred_element_type=jnp.float32)
        hidden = (hidden * gate_flat[picked][:, None] * silu_slope(saved)).astype(jnp.bfloat16)
        back = jnp.dot(hidden, w_in[slot].T, preferred_element_type=jnp.float32).astype(jnp.bfloat16)
        back = jnp.where(valid[:, None], back.astype(jnp.float32), jnp.float32(0.0))
        return running.at[tokens_picked].add(back), None

    running, _ = lax.scan(one_piece, jnp.zeros((TOKENS, D), jnp.float32), jnp.arange(SLOTS, dtype=jnp.int32))
    token_grads = running.astype(jnp.bfloat16)
    block_of = jnp.arange(TOKENS, dtype=jnp.int32) // PAIR_TOK
    target = jnp.where(tile_slot >= 0, block_of * VIS_PAIR + tile_slot, PARTDEV * VIS_DEV).astype(jnp.int32)
    visual = jnp.zeros((PARTDEV * VIS_DEV, D), jnp.bfloat16).at[target].set(token_grads, mode="drop")
    adapter_grad = (visual.astype(jnp.float32) * gelu_slope(adapter_pre.astype(jnp.float32))).astype(jnp.bfloat16)
    shuffled = jnp.dot(adapter_grad, w_adapt.T, preferred_element_type=jnp.float32)
    patch_grads = shuffled.reshape(PARTDEV, TILE_R, TILE_C, 2, 2, SIGW).transpose(0, 1, 3, 2, 4, 5)
    patch_grads = patch_grads.reshape(PARTDEV * 2 * TILE_R, 2 * TILE_C * SIGW)
    return token_grads, patch_grads
```

```python
import jax
import jax.numpy as jnp
from jax import lax
from jax.experimental import pallas as pl
from jax.experimental.pallas import tpu as pltpu
from jax.sharding import PartitionSpec as P

EXPERTS = 64
TOP = 6
SIGW = 576
TILE_R = 8


def silu_slope(value):
    sigma = jax.nn.sigmoid(value)
    return sigma * (1.0 + value * (1.0 - sigma))


def gelu_slope(value):
    normal_cdf = 0.5 * (1.0 + lax.erf(value * 0.7071067811865476))
    return normal_cdf + value * jnp.exp(-0.5 * value * value) * 0.3989422804014327


def row_exchange(out_grad, gates, routes, w_in, w_out, expert_pre):
    axis_count = lax.axis_size("expert")
    tok_count, feature_width = out_grad.shape
    top_count = routes.shape[1]
    local_experts = w_in.shape[0]
    replicas = max(1, axis_count // EXPERTS)
    slot_depth = expert_pre.shape[2]
    slot_total = axis_count * local_experts * slot_depth
    flat_routes = routes.reshape(-1)
    expert_hot = (flat_routes[:, None] == jnp.arange(EXPERTS, dtype=jnp.int32)[None, :]).astype(
        jnp.int32
    )
    earlier = jnp.cumsum(expert_hot, axis=0) - expert_hot
    row_rank = jnp.sum(earlier * expert_hot, axis=1)
    slot_range = jnp.arange(slot_total, dtype=jnp.int32)[None, :]
    row_hits = jnp.zeros((tok_count * top_count, slot_total), jnp.bool_)
    for piece in range(replicas):
        slot_id = (flat_routes + piece * EXPERTS) * slot_depth + row_rank
        row_hits = jnp.logical_or(row_hits, slot_id[:, None] == slot_range)
    token_slot = row_hits.reshape(tok_count, top_count, slot_total)
    placing = jnp.sum(token_slot.astype(jnp.bfloat16), axis=1)
    gate_slot = jnp.sum(
        jnp.where(token_slot, gates.astype(jnp.float32)[:, :, None], 0.0), axis=(0, 1)
    ).astype(jnp.bfloat16)
    send_rows = lax.dot_general(
        placing, out_grad, (((0,), (0,)), ((), ())), preferred_element_type=jnp.float32
    )
    send_rows = send_rows.astype(jnp.bfloat16).reshape(
        axis_count, local_experts, slot_depth, feature_width
    )
    gate_slot = gate_slot.reshape(axis_count, local_experts, slot_depth)
    recv_rows, recv_gates = (
        lax.all_to_all(send_rows, "expert", split_axis=0, concat_axis=0, tiled=True),
        lax.all_to_all(gate_slot, "expert", split_axis=0, concat_axis=0, tiled=True),
    )
    full_in, full_out = (
        lax.all_gather(w_in, "dp", axis=1, tiled=True),
        lax.all_gather(w_out, "dp", axis=2, tiled=True),
    )
    hidden_grad = jnp.einsum(
        "nlcd,lfd->nlcf", recv_rows, full_out, preferred_element_type=jnp.float32
    )
    hidden_grad = (
        hidden_grad
        * recv_gates.astype(jnp.float32)[..., None]
        * silu_slope(expert_pre.astype(jnp.float32))
    )
    hidden_grad = hidden_grad.astype(jnp.bfloat16)
    row_grad = jnp.einsum(
        "nlcf,ldf->nlcd", hidden_grad, full_in, preferred_element_type=jnp.float32
    ).astype(jnp.bfloat16)
    returned = lax.all_to_all(row_grad, "expert", split_axis=0, concat_axis=0, tiled=True)
    return jnp.dot(
        placing, returned.reshape(slot_total, feature_width), preferred_element_type=jnp.float32
    ).astype(jnp.bfloat16)


PAD = 16


def expert_kernel(first_ref, rows_in, info, w_out, w_in, pre, out, placed, rows, hidden, back, scale):
    sources, tokens, _ = rows_in.shape
    experts = pl.num_programs(0)
    step = pl.program_id(0)
    slots = placed.shape[2]
    depth = pre.shape[2]

    @pl.when(step == 0)
    def _():
        first = first_ref[0]
        slot = lax.broadcasted_iota(jnp.int32, (tokens, slots), 1)
        expert = (first + slot // PAD).astype(jnp.float32)
        rank_of = (slot % PAD).astype(jnp.float32)
        later = lax.broadcasted_iota(jnp.int32, (tokens, tokens), 0)
        before = (lax.broadcasted_iota(jnp.int32, (tokens, tokens), 1) < later).astype(jnp.bfloat16)
        for n in range(sources):
            named = jnp.zeros((tokens, slots), jnp.float32)
            weight = jnp.zeros((tokens, slots), jnp.float32)
            table = info[n].astype(jnp.float32)
            for k in range(TOP):
                same = (table[:, TOP + k : TOP + k + 1] == expert).astype(jnp.float32)
                named = named + same
                weight = weight + same * table[:, k : k + 1]
            rank = jnp.dot(before, named.astype(jnp.bfloat16), preferred_element_type=jnp.float32)
            chosen = jnp.where(rank == rank_of, named, 0.0)
            placed[n] = chosen.astype(jnp.bfloat16)
            scale[n] = jnp.sum((chosen * weight).T, axis=1, keepdims=True)
            rows[n] = lax.dot_general(
                chosen.astype(jnp.bfloat16),
                rows_in[n],
                (((0,), (0,)), ((), ())),
                preferred_element_type=jnp.float32,
            ).astype(jnp.bfloat16)

    at = pl.ds(pl.multiple_of(step * PAD, PAD), PAD)
    taken = jnp.concatenate([rows[n, at, :] for n in range(sources)], axis=0)
    product = lax.dot_general(
        taken, w_out[0], (((1,), (1,)), ((), ())), preferred_element_type=jnp.float32
    )
    for n in range(sources):
        slope = silu_slope(pre[n, 0].astype(jnp.float32))
        part = product[n * PAD : n * PAD + depth] * scale[n, pl.ds(step * PAD, depth), :] * slope
        part = jnp.concatenate([part, jnp.zeros((PAD - depth, part.shape[1]), jnp.float32)], axis=0)
        hidden[n * PAD : (n + 1) * PAD] = part.astype(jnp.bfloat16)
    grads = lax.dot_general(
        hidden[...], w_in[0], (((1,), (1,)), ((), ())), preferred_element_type=jnp.float32
    ).astype(jnp.bfloat16)
    for n in range(sources):
        back[n, at, :] = grads[n * PAD : (n + 1) * PAD]

    @pl.when(step == experts - 1)
    def _():
        for n in range(sources):
            out[n] = jnp.dot(placed[n], back[n], preferred_element_type=jnp.float32).astype(jnp.bfloat16)


def block_exchange(out_grad, gates, routes, w_in, w_out, expert_pre):
    axis_count = lax.axis_size("expert")
    tok_count, width = out_grad.shape
    experts, _, fw = w_out.shape[0], w_out.shape[1], w_out.shape[1]
    depth = expert_pre.shape[2]
    info = jnp.concatenate([gates, routes.astype(jnp.bfloat16)], axis=1)
    info = jnp.pad(info, ((0, 0), (0, 128 - 2 * TOP)))
    info = lax.all_gather(info, "expert", axis=0)
    rows_in = lax.all_gather(out_grad, "expert", axis=0)
    full_out = lax.all_gather(w_out, "dp", axis=2, tiled=True)
    full_in = lax.all_gather(w_in, "dp", axis=1, tiled=True)
    first = (lax.axis_index("expert") * experts).astype(jnp.int32).reshape(1)
    slots = experts * PAD
    whole = lambda *shape: pl.BlockSpec(shape, lambda s: (0,) * len(shape))
    partial = pl.pallas_call(
        expert_kernel,
        grid=(experts,),
        out_shape=jax.ShapeDtypeStruct((axis_count, tok_count, width), jnp.bfloat16),
        in_specs=[
            pl.BlockSpec(memory_space=pltpu.SMEM),
            whole(axis_count, tok_count, width),
            whole(axis_count, tok_count, 128),
            pl.BlockSpec((1, fw, width), lambda s: (s, 0, 0)),
            pl.BlockSpec((1, width, fw), lambda s: (s, 0, 0)),
            pl.BlockSpec((axis_count, 1, depth, fw), lambda s: (0, s, 0, 0)),
        ],
        out_specs=whole(axis_count, tok_count, width),
        scratch_shapes=[
            pltpu.VMEM((axis_count, tok_count, slots), jnp.bfloat16),
            pltpu.VMEM((axis_count, slots, width), jnp.bfloat16),
            pltpu.VMEM((axis_count * PAD, fw), jnp.bfloat16),
            pltpu.VMEM((axis_count, slots, width), jnp.bfloat16),
            pltpu.VMEM((axis_count, slots, 1), jnp.float32),
        ],
        compiler_params=pltpu.CompilerParams(vmem_limit_bytes=50 << 20),
    )(first, rows_in, info, full_out, full_in, expert_pre)
    return lax.psum_scatter(partial.reshape(axis_count * tok_count, width), "expert", scatter_dimension=0, tiled=True)


def body(out_grad, gates, routes, tile_slot, w_in, w_out, expert_pre, adapter_pre, w_adapt):
    core_count = lax.axis_size("dp")
    feature_width = out_grad.shape[1]
    if lax.axis_size("expert") <= 8 and out_grad.shape[0] % 128 == 0 and expert_pre.shape[2] <= PAD:
        exchange = block_exchange
    else:
        exchange = row_exchange
    token_grads = exchange(out_grad, gates, routes, w_in, w_out, expert_pre)
    vis_count = adapter_pre.shape[0]
    owner_hot = (
        tile_slot[None, :] == jnp.arange(core_count * vis_count, dtype=jnp.int32)[:, None]
    ).astype(jnp.bfloat16)
    outgoing = jnp.dot(owner_hot, token_grads, preferred_element_type=jnp.float32).astype(
        jnp.bfloat16
    )
    incoming = lax.all_to_all(
        outgoing.reshape(core_count, vis_count, feature_width),
        "dp",
        split_axis=0,
        concat_axis=0,
        tiled=True,
    )
    visual_grad = jnp.sum(incoming.astype(jnp.float32), axis=0)
    adapter_grad = (visual_grad * gelu_slope(adapter_pre.astype(jnp.float32))).astype(jnp.bfloat16)
    shuffled = lax.dot_general(
        adapter_grad,
        lax.all_gather(w_adapt, ("expert", "dp"), axis=0, tiled=True),
        (((1,), (1,)), ((), ())),
        preferred_element_type=jnp.float32,
    )
    tile_cols = vis_count // TILE_R
    patch_grads = shuffled.reshape(TILE_R, tile_cols, 2, 2, SIGW).transpose(0, 2, 1, 3, 4)
    patch_grads = patch_grads.reshape(2 * TILE_R, 2 * tile_cols * SIGW)
    return (token_grads, patch_grads)


def solution(mesh):
    placed = (
        P(("groups", "expert", "dp"), None),
        P(("groups", "expert", "dp"), None),
        P(("groups", "expert", "dp"), None),
        P(("groups", "expert", "dp")),
        P("expert", "dp", None),
        P("expert", None, "dp"),
        P(("groups", "expert", "dp"), None, None, None),
        P(("groups", "expert", "dp"), None),
        P(("expert", "dp"), None),
    )
    return jax.shard_map(
        body,
        mesh=mesh,
        in_specs=placed,
        out_specs=(P(("groups", "expert", "dp"), None), P(("groups", "expert", "dp"), None)),
        check_vma=False,
    )
```

```python
import jax
import jax.numpy as jnp
from jax import lax
from jax.experimental import pallas as pl
from jax.experimental.pallas import tpu as pltpu
from jax.sharding import PartitionSpec as P

EXPERTS = 64
TOP = 6
SIGW = 576
TILE_R = 8


def silu_slope(value):
    sigma = jax.nn.sigmoid(value)
    return sigma * (1.0 + value * (1.0 - sigma))


def gelu_slope(value):
    normal_cdf = 0.5 * (1.0 + lax.erf(value * 0.7071067811865476))
    return normal_cdf + value * jnp.exp(-0.5 * value * value) * 0.3989422804014327


def row_exchange(out_grad, gates, routes, tile_slot, w_in, w_out, expert_pre, vis_count):
    axis_count = lax.axis_size("expert")
    core_count = lax.axis_size("dp")
    tok_count, feature_width = out_grad.shape
    top_count = routes.shape[1]
    local_experts = w_in.shape[0]
    replicas = max(1, axis_count // EXPERTS)
    slot_depth = expert_pre.shape[2]
    slot_total = axis_count * local_experts * slot_depth
    flat_routes = routes.reshape(-1)
    expert_hot = (flat_routes[:, None] == jnp.arange(EXPERTS, dtype=jnp.int32)[None, :]).astype(
        jnp.int32
    )
    earlier = jnp.cumsum(expert_hot, axis=0) - expert_hot
    row_rank = jnp.sum(earlier * expert_hot, axis=1)
    slot_range = jnp.arange(slot_total, dtype=jnp.int32)[None, :]
    row_hits = jnp.zeros((tok_count * top_count, slot_total), jnp.bool_)
    for piece in range(replicas):
        slot_id = (flat_routes + piece * EXPERTS) * slot_depth + row_rank
        row_hits = jnp.logical_or(row_hits, slot_id[:, None] == slot_range)
    token_slot = row_hits.reshape(tok_count, top_count, slot_total)
    placing = jnp.sum(token_slot.astype(jnp.bfloat16), axis=1)
    gate_slot = jnp.sum(
        jnp.where(token_slot, gates.astype(jnp.float32)[:, :, None], 0.0), axis=(0, 1)
    ).astype(jnp.bfloat16)
    send_rows = lax.dot_general(
        placing, out_grad, (((0,), (0,)), ((), ())), preferred_element_type=jnp.float32
    )
    send_rows = send_rows.astype(jnp.bfloat16).reshape(
        axis_count, local_experts, slot_depth, feature_width
    )
    gate_slot = gate_slot.reshape(axis_count, local_experts, slot_depth)
    recv_rows, recv_gates = (
        lax.all_to_all(send_rows, "expert", split_axis=0, concat_axis=0, tiled=True),
        lax.all_to_all(gate_slot, "expert", split_axis=0, concat_axis=0, tiled=True),
    )
    full_in, full_out = (
        lax.all_gather(w_in, "dp", axis=1, tiled=True),
        lax.all_gather(w_out, "dp", axis=2, tiled=True),
    )
    hidden_grad = jnp.einsum(
        "nlcd,lfd->nlcf", recv_rows, full_out, preferred_element_type=jnp.float32
    )
    hidden_grad = (
        hidden_grad
        * recv_gates.astype(jnp.float32)[..., None]
        * silu_slope(expert_pre.astype(jnp.float32))
    )
    hidden_grad = hidden_grad.astype(jnp.bfloat16)
    row_grad = jnp.einsum(
        "nlcf,ldf->nlcd", hidden_grad, full_in, preferred_element_type=jnp.float32
    ).astype(jnp.bfloat16)
    returned = lax.all_to_all(row_grad, "expert", split_axis=0, concat_axis=0, tiled=True)
    token_grads = jnp.dot(
        placing, returned.reshape(slot_total, feature_width), preferred_element_type=jnp.float32
    ).astype(jnp.bfloat16)
    owner_hot = (
        tile_slot[None, :] == jnp.arange(core_count * vis_count, dtype=jnp.int32)[:, None]
    ).astype(jnp.bfloat16)
    outgoing = jnp.dot(owner_hot, token_grads, preferred_element_type=jnp.float32).astype(
        jnp.bfloat16
    )
    incoming = lax.all_to_all(
        outgoing.reshape(core_count, vis_count, feature_width),
        "dp",
        split_axis=0,
        concat_axis=0,
        tiled=True,
    )
    return token_grads, jnp.sum(incoming.astype(jnp.float32), axis=0)


PAD = 16
MESH = pl.DeviceIdType.MESH


def seat_of(index, count):
    odd, half = index % 2, index // 2
    return half * (1 - odd) + (count - 1 - half) * odd


def index_of(seat, count):
    back = seat // (count // 2)
    return 2 * seat * (1 - back) + (2 * (count - 1 - seat) + 1) * back


def exchange_kernel(
    x, info, slot_row, pre, w_out, w_in, token_out, visual_out,
    xs, infos, wo, wi, placed, rows, back, scale, hidden, outbox, inbox, vis_send, vis_recv,
    x_send, x_recv, i_send, i_recv, w_local, w_send, w_recv, r_send, r_recv, v_send, v_recv,
):
    count, tokens, width = xs.shape
    experts, fw, half_width = wo.shape[1], wo.shape[2], wo.shape[3]
    slots = experts * PAD
    depth = pre.shape[2]
    half = tokens // 2
    far = count // 2
    core = lax.axis_index("dp")
    expert_index = lax.axis_index("expert")
    seat = seat_of(expert_index, count)
    right = {"expert": index_of((seat + 1) % count, count)}
    left = {"expert": index_of((seat + count - 1) % count, count)}
    sibling = {"dp": 1 - core}

    def own_weight(l, which):
        source, target = ((w_out, wo), (w_in, wi))[which]
        return pltpu.make_async_copy(source.at[l], target.at[core, l], w_local.at[which, l])

    def sent_weight(l, which):
        source, target = ((w_out, wo), (w_in, wi))[which]
        return pltpu.make_async_remote_copy(
            source.at[l], target.at[core, l], w_send.at[which, l], w_recv.at[which, l],
            device_id=sibling, device_id_type=MESH,
        )

    barrier = pltpu.get_barrier_semaphore()
    for other in (left, right, sibling):
        pl.semaphore_signal(barrier, inc=1, device_id=other, device_id_type=MESH)
    pl.semaphore_wait(barrier, 3)

    def ring(step, way):
        come, go = (step - 1, step) if way == 0 else ((count - step + 1) % count, count - step)
        block = x if step == 1 else xs.at[come]
        note = info if step == 1 else infos.at[come]
        to = (right, left)[way]
        copies = []
        at = pl.ds(way * half, half) if step == far else pl.ds(0, tokens)
        copies.append(
            pltpu.make_async_remote_copy(
                block.at[at], xs.at[go, at], x_send.at[way, step], x_recv.at[way, step],
                device_id=to, device_id_type=MESH,
            )
        )
        if step < far or way == 0:
            copies.append(
                pltpu.make_async_remote_copy(
                    note, infos.at[go], i_send.at[way, step], i_recv.at[way, step],
                    device_id=to, device_id_type=MESH,
                )
            )
        return copies

    sends = [ring(1, 0), ring(1, 1)]
    for copies in sends:
        for copy in copies:
            copy.start()

    @pl.loop(0, experts)
    def _(l):
        for which in range(2):
            sent_weight(l, which).start()
            own_weight(l, which).start()

    slot = lax.broadcasted_iota(jnp.int32, (slots, tokens), 0)
    expert = (expert_index * experts + slot // PAD).astype(jnp.float32)
    rank_of = (slot % PAD).astype(jnp.float32)
    before = (
        lax.broadcasted_iota(jnp.int32, (tokens, tokens), 0)
        < lax.broadcasted_iota(jnp.int32, (tokens, tokens), 1)
    ).astype(jnp.bfloat16)

    def take(offset):
        block = x if offset == 0 else xs.at[offset]
        table = (info if offset == 0 else infos.at[offset])[...].astype(jnp.float32)
        named = jnp.zeros((slots, tokens), jnp.float32)
        weight = jnp.zeros((slots, tokens), jnp.float32)
        for k in range(TOP):
            same = (table[TOP + k : TOP + k + 1, :] == expert).astype(jnp.float32)
            named = named + same
            weight = weight + same * table[k : k + 1, :]
        rank = jnp.dot(named.astype(jnp.bfloat16), before, preferred_element_type=jnp.float32)
        chosen = jnp.where(rank == rank_of, named, 0.0)
        placed[offset] = chosen.astype(jnp.bfloat16)
        scale[offset] = jnp.sum(chosen * weight, axis=1, keepdims=True)
        rows[offset] = jnp.dot(
            chosen.astype(jnp.bfloat16), block[...], preferred_element_type=jnp.float32
        ).astype(jnp.bfloat16)

    take(0)
    for step in range(1, far + 1):
        for copies in sends:
            for copy in copies:
                copy.wait()
        if step < far:
            sends = [ring(step + 1, 0), ring(step + 1, 1)]
            for copies in sends:
                for copy in copies:
                    copy.start()
        take(step)
        if step < far:
            take(count - step)

    @pl.loop(0, experts)
    def _(l):
        for which in range(2):
            own_weight(l, which).wait()
            sent_weight(l, which).wait()
        at = pl.ds(pl.multiple_of(l * PAD, PAD), PAD)
        taken = jnp.concatenate([rows[o, at, :] for o in range(count)], axis=0)
        product = lax.dot_general(
            taken[:, :half_width], wo[0, l], (((1,), (1,)), ((), ())), preferred_element_type=jnp.float32
        ) + lax.dot_general(
            taken[:, half_width:], wo[1, l], (((1,), (1,)), ((), ())), preferred_element_type=jnp.float32
        )
        for o in range(count):
            source = index_of((seat + count - o) % count, count)
            slope = silu_slope(pre[source, l].astype(jnp.float32))
            part = product[o * PAD : o * PAD + depth] * scale[o, at, :][:depth] * slope
            part = jnp.concatenate([part, jnp.zeros((PAD - depth, fw), jnp.float32)], axis=0)
            hidden[o * PAD : (o + 1) * PAD] = part.astype(jnp.bfloat16)
        for c in range(2):
            grads = lax.dot_general(
                hidden[...], wi[c, l], (((1,), (1,)), ((), ())), preferred_element_type=jnp.float32
            ).astype(jnp.bfloat16)
            for o in range(count):
                back[o, at, c * half_width : (c + 1) * half_width] = grads[o * PAD : (o + 1) * PAD]

    def total(offset):
        return lax.dot_general(
            placed[offset], back[offset], (((0,), (0,)), ((), ())), preferred_element_type=jnp.float32
        )

    def hop(step, way):
        at = pl.ds(way * half, half) if step == 1 else pl.ds(0, tokens)
        return pltpu.make_async_remote_copy(
            outbox.at[way, step - 1, at], inbox.at[way, step - 1, at],
            r_send.at[way, step - 1], r_recv.at[way, step - 1],
            device_id=(right, left)[way], device_id_type=MESH,
        )

    outbox[0, 0] = total(far).astype(jnp.bfloat16)
    outbox[1, 0, half:] = outbox[0, 0, half:]
    hops = [hop(1, 0), hop(1, 1)]
    for copy in hops:
        copy.start()
    for step in range(2, far + 1):
        distance = far + 1 - step
        mine = [total(count - distance), total(distance)]
        later = []
        for way in range(2):
            hops[way].wait()
            if step == 2:
                at = slice(way * half, (way + 1) * half)
                rest = slice((1 - way) * half, (2 - way) * half)
                outbox[way, 1, at] = (
                    mine[way][at] + inbox[way, 0, at].astype(jnp.float32)
                ).astype(jnp.bfloat16)
                outbox[way, 1, rest] = mine[way][rest].astype(jnp.bfloat16)
            else:
                outbox[way, step - 1] = (
                    mine[way] + inbox[way, step - 2].astype(jnp.float32)
                ).astype(jnp.bfloat16)
            copy = hop(step, way)
            copy.start()
            later.append(copy)
        hops = later
    result = total(0)
    for way in range(2):
        hops[way].wait()
        result = result + inbox[way, far - 1].astype(jnp.float32)
    result = result.astype(jnp.bfloat16)
    token_out[...] = result

    vis = visual_out.shape[0]
    row = lax.broadcasted_iota(jnp.int32, (vis, tokens), 0)
    theirs = (slot_row[...] == row + (1 - core) * vis).astype(jnp.bfloat16)
    vis_send[...] = jnp.dot(theirs, result, preferred_element_type=jnp.float32).astype(jnp.bfloat16)
    copy = pltpu.make_async_remote_copy(
        vis_send, vis_recv, v_send, v_recv, device_id=sibling, device_id_type=MESH
    )
    copy.start()
    ours = (slot_row[...] == row + core * vis).astype(jnp.bfloat16)
    kept = jnp.dot(ours, result, preferred_element_type=jnp.float32)
    copy.wait()
    visual_out[...] = (kept + vis_recv[...].astype(jnp.float32)).astype(jnp.bfloat16)


def block_exchange(out_grad, gates, routes, tile_slot, w_in, w_out, expert_pre, vis_count):
    count = lax.axis_size("expert")
    tokens, width = out_grad.shape
    experts, fw, half_width = w_out.shape
    info = jnp.concatenate([gates.T, routes.T.astype(jnp.bfloat16)], axis=0)
    info = jnp.pad(info, ((0, PAD - 2 * TOP), (0, 0)))
    slots = experts * PAD
    bf16 = jnp.bfloat16
    dma = pltpu.SemaphoreType.DMA
    far = count // 2
    vmem = pl.BlockSpec(memory_space=pltpu.VMEM)
    token_grads, visual = pl.pallas_call(
        exchange_kernel,
        out_shape=(
            jax.ShapeDtypeStruct((tokens, width), bf16),
            jax.ShapeDtypeStruct((vis_count, width), bf16),
        ),
        in_specs=[vmem] * 4 + [pl.BlockSpec(memory_space=pl.ANY)] * 2,
        out_specs=(vmem, vmem),
        scratch_shapes=[
            pltpu.VMEM((count, tokens, width), bf16),
            pltpu.VMEM((count, PAD, tokens), bf16),
            pltpu.VMEM((2, experts, fw, half_width), bf16),
            pltpu.VMEM((2, experts, half_width, fw), bf16),
            pltpu.VMEM((count, slots, tokens), bf16),
            pltpu.VMEM((count, slots, width), bf16),
            pltpu.VMEM((count, slots, width), bf16),
            pltpu.VMEM((count, slots, 1), jnp.float32),
            pltpu.VMEM((count * PAD, fw), bf16),
            pltpu.VMEM((2, far, tokens, width), bf16),
            pltpu.VMEM((2, far, tokens, width), bf16),
            pltpu.VMEM((vis_count, width), bf16),
            pltpu.VMEM((vis_count, width), bf16),
            dma((2, far + 1)), dma((2, far + 1)), dma((2, far + 1)), dma((2, far + 1)),
            dma((2, experts)), dma((2, experts)), dma((2, experts)),
            dma((2, far)), dma((2, far)), dma, dma,
        ],
        compiler_params=pltpu.CompilerParams(
            collective_id=0, has_side_effects=True, vmem_limit_bytes=58 << 20
        ),
        cost_estimate=pl.CostEstimate(
            flops=4 * experts * count * PAD * width * fw, bytes_accessed=4 * experts * width * fw, transcendentals=0
        ),
    )(out_grad, info, tile_slot.reshape(1, tokens), expert_pre, w_out, w_in)
    return token_grads, visual.astype(jnp.float32)


def body(out_grad, gates, routes, tile_slot, w_in, w_out, expert_pre, adapter_pre, w_adapt):
    vis_count = adapter_pre.shape[0]
    if lax.axis_size("expert") == 8 and out_grad.shape[0] == 128 and expert_pre.shape[2] <= PAD:
        exchange = block_exchange
    else:
        exchange = row_exchange
    token_grads, visual_grad = exchange(
        out_grad, gates, routes, tile_slot, w_in, w_out, expert_pre, vis_count
    )
    adapter_grad = (visual_grad * gelu_slope(adapter_pre.astype(jnp.float32))).astype(jnp.bfloat16)
    shuffled = lax.dot_general(
        adapter_grad,
        lax.all_gather(w_adapt, ("expert", "dp"), axis=0, tiled=True),
        (((1,), (1,)), ((), ())),
        preferred_element_type=jnp.float32,
    )
    tile_cols = vis_count // TILE_R
    patch_grads = shuffled.reshape(TILE_R, tile_cols, 2, 2, SIGW).transpose(0, 2, 1, 3, 4)
    patch_grads = patch_grads.reshape(2 * TILE_R, 2 * tile_cols * SIGW)
    return (token_grads, patch_grads)


def solution(mesh):
    placed = (
        P(("groups", "expert", "dp"), None),
        P(("groups", "expert", "dp"), None),
        P(("groups", "expert", "dp"), None),
        P(("groups", "expert", "dp")),
        P("expert", "dp", None),
        P("expert", None, "dp"),
        P(("groups", "expert", "dp"), None, None, None),
        P(("groups", "expert", "dp"), None),
        P(("expert", "dp"), None),
    )
    return jax.shard_map(
        body,
        mesh=mesh,
        in_specs=placed,
        out_specs=(P(("groups", "expert", "dp"), None), P(("groups", "expert", "dp"), None)),
        check_vma=False,
    )
```

```python
import jax
import jax.numpy as jnp
from jax import lax
from jax.experimental import pallas as pl
from jax.experimental.pallas import tpu as pltpu
from jax.sharding import PartitionSpec as P

EXPERTS = 64
TOP = 6
SIGW = 576
TILE_R = 8


def silu_slope(value):
    sigma = jax.nn.sigmoid(value)
    return sigma * (1.0 + value * (1.0 - sigma))


def gelu_slope(value):
    normal_cdf = 0.5 * (1.0 + lax.erf(value * 0.7071067811865476))
    return normal_cdf + value * jnp.exp(-0.5 * value * value) * 0.3989422804014327


def row_exchange(out_grad, gates, routes, tile_slot, w_in, w_out, expert_pre, vis_count):
    axis_count = lax.axis_size("expert")
    core_count = lax.axis_size("dp")
    tok_count, feature_width = out_grad.shape
    top_count = routes.shape[1]
    local_experts = w_in.shape[0]
    replicas = max(1, axis_count // EXPERTS)
    slot_depth = expert_pre.shape[2]
    slot_total = axis_count * local_experts * slot_depth
    flat_routes = routes.reshape(-1)
    expert_hot = (flat_routes[:, None] == jnp.arange(EXPERTS, dtype=jnp.int32)[None, :]).astype(
        jnp.int32
    )
    earlier = jnp.cumsum(expert_hot, axis=0) - expert_hot
    row_rank = jnp.sum(earlier * expert_hot, axis=1)
    slot_range = jnp.arange(slot_total, dtype=jnp.int32)[None, :]
    row_hits = jnp.zeros((tok_count * top_count, slot_total), jnp.bool_)
    for piece in range(replicas):
        slot_id = (flat_routes + piece * EXPERTS) * slot_depth + row_rank
        row_hits = jnp.logical_or(row_hits, slot_id[:, None] == slot_range)
    token_slot = row_hits.reshape(tok_count, top_count, slot_total)
    placing = jnp.sum(token_slot.astype(jnp.bfloat16), axis=1)
    gate_slot = jnp.sum(
        jnp.where(token_slot, gates.astype(jnp.float32)[:, :, None], 0.0), axis=(0, 1)
    ).astype(jnp.bfloat16)
    send_rows = lax.dot_general(
        placing, out_grad, (((0,), (0,)), ((), ())), preferred_element_type=jnp.float32
    )
    send_rows = send_rows.astype(jnp.bfloat16).reshape(
        axis_count, local_experts, slot_depth, feature_width
    )
    gate_slot = gate_slot.reshape(axis_count, local_experts, slot_depth)
    recv_rows, recv_gates = (
        lax.all_to_all(send_rows, "expert", split_axis=0, concat_axis=0, tiled=True),
        lax.all_to_all(gate_slot, "expert", split_axis=0, concat_axis=0, tiled=True),
    )
    full_in, full_out = (
        lax.all_gather(w_in, "dp", axis=1, tiled=True),
        lax.all_gather(w_out, "dp", axis=2, tiled=True),
    )
    hidden_grad = jnp.einsum(
        "nlcd,lfd->nlcf", recv_rows, full_out, preferred_element_type=jnp.float32
    )
    hidden_grad = (
        hidden_grad
        * recv_gates.astype(jnp.float32)[..., None]
        * silu_slope(expert_pre.astype(jnp.float32))
    )
    hidden_grad = hidden_grad.astype(jnp.bfloat16)
    row_grad = jnp.einsum(
        "nlcf,ldf->nlcd", hidden_grad, full_in, preferred_element_type=jnp.float32
    ).astype(jnp.bfloat16)
    returned = lax.all_to_all(row_grad, "expert", split_axis=0, concat_axis=0, tiled=True)
    token_grads = jnp.dot(
        placing, returned.reshape(slot_total, feature_width), preferred_element_type=jnp.float32
    ).astype(jnp.bfloat16)
    owner_hot = (
        tile_slot[None, :] == jnp.arange(core_count * vis_count, dtype=jnp.int32)[:, None]
    ).astype(jnp.bfloat16)
    outgoing = jnp.dot(owner_hot, token_grads, preferred_element_type=jnp.float32).astype(
        jnp.bfloat16
    )
    incoming = lax.all_to_all(
        outgoing.reshape(core_count, vis_count, feature_width),
        "dp",
        split_axis=0,
        concat_axis=0,
        tiled=True,
    )
    return token_grads, jnp.sum(incoming.astype(jnp.float32), axis=0)


PAD = 16
MESH = pl.DeviceIdType.MESH


def seat_of(index, count):
    odd, half = index % 2, index // 2
    return half * (1 - odd) + (count - 1 - half) * odd


def index_of(seat, count):
    back = seat // (count // 2)
    return 2 * seat * (1 - back) + (2 * (count - 1 - seat) + 1) * back


def exchange_kernel(
    x, info, slot_row, pre, slope_in, w_out, w_in, w_adapt, token_out, shuffled_out,
    xs, infos, wo, wi, placed, rows, back, scale, hidden, outbox, inbox, vis_send, vis_recv, wa,
    x_send, x_recv, i_send, i_recv, w_local, w_send, w_recv, r_send, r_recv, v_send, v_recv,
    a_own, a_send, a_recv, y_send, y_recv, s_send, s_recv,
):
    count, tokens, width = xs.shape
    experts, fw, half_width = wo.shape[1], wo.shape[2], wo.shape[3]
    slots = experts * PAD
    depth = pre.shape[2]
    half = tokens // 2
    far = count // 2
    core = lax.axis_index("dp")
    expert_index = lax.axis_index("expert")
    seat = seat_of(expert_index, count)
    right = {"expert": index_of((seat + 1) % count, count)}
    left = {"expert": index_of((seat + count - 1) % count, count)}
    sibling = {"dp": 1 - core}
    group = lax.axis_index("groups")
    twin = {"groups": 1 - group}
    shard = w_adapt.shape[0]
    cut = (shard // 2 + PAD - 1) // PAD * PAD

    def columns(which):
        return pl.ds(pl.multiple_of(which * half_width, 128), half_width)

    def shard_at(offset, start=0, size=None):
        owner = index_of((seat + count - offset) % count, count)
        first = pl.multiple_of((owner * 2 + core) * shard + start, PAD)
        return pl.ds(first, shard if size is None else size)

    def adapt_ring(step, way):
        offset = step - 1 if way == 0 else (count - step + 1) % count
        start, size = (0, shard) if step < far else ((0, cut), (cut, shard - cut))[way]
        place = wa.at[shard_at(offset, start, size), columns(group)]
        source = w_adapt.at[pl.ds(start, size), columns(group)] if step == 1 else place
        return pltpu.make_async_remote_copy(
            source, place, a_send.at[way, step], a_recv.at[way, step],
            device_id=(right, left)[way], device_id_type=MESH,
        )

    def adapt_twin(offset):
        place = wa.at[shard_at(offset), columns(group)]
        return pltpu.make_async_remote_copy(
            place, place, y_send.at[offset], y_recv.at[offset], device_id=twin, device_id_type=MESH
        )

    def adapt_sibling(offset, mine):
        which = group if mine == 0 else 1 - group
        place = wa.at[shard_at(offset), columns(which)]
        source = w_adapt.at[:, columns(which)] if offset == 0 else place
        return pltpu.make_async_remote_copy(
            source, place, s_send.at[mine, offset], s_recv.at[mine, offset],
            device_id=sibling, device_id_type=MESH,
        )

    adapt_own = pltpu.make_async_copy(w_adapt, wa.at[shard_at(0)], a_own)

    def own_weight(l, which):
        source, target = ((w_out, wo), (w_in, wi))[which]
        return pltpu.make_async_copy(source.at[l], target.at[core, l], w_local.at[which, l])

    def sent_weight(l, which):
        source, target = ((w_out, wo), (w_in, wi))[which]
        return pltpu.make_async_remote_copy(
            source.at[l], target.at[core, l], w_send.at[which, l], w_recv.at[which, l],
            device_id=sibling, device_id_type=MESH,
        )

    barrier = pltpu.get_barrier_semaphore()
    for other in (left, right, sibling, twin):
        pl.semaphore_signal(barrier, inc=1, device_id=other, device_id_type=MESH)
    pl.semaphore_wait(barrier, 4)

    def ring(step, way):
        come, go = (step - 1, step) if way == 0 else ((count - step + 1) % count, count - step)
        block = x if step == 1 else xs.at[come]
        note = info if step == 1 else infos.at[come]
        to = (right, left)[way]
        copies = []
        at = pl.ds(way * half, half) if step == far else pl.ds(0, tokens)
        copies.append(
            pltpu.make_async_remote_copy(
                block.at[at], xs.at[go, at], x_send.at[way, step], x_recv.at[way, step],
                device_id=to, device_id_type=MESH,
            )
        )
        if step < far or way == 0:
            copies.append(
                pltpu.make_async_remote_copy(
                    note, infos.at[go], i_send.at[way, step], i_recv.at[way, step],
                    device_id=to, device_id_type=MESH,
                )
            )
        return copies

    sends = [ring(1, 0), ring(1, 1)]
    for copies in sends:
        for copy in copies:
            copy.start()

    @pl.loop(0, experts)
    def _(l):
        for which in range(2):
            sent_weight(l, which).start()
            own_weight(l, which).start()

    adapt_own.start()
    for mine in range(2):
        adapt_sibling(0, mine).start()

    slot = lax.broadcasted_iota(jnp.int32, (slots, tokens), 0)
    expert = (expert_index * experts + slot // PAD).astype(jnp.float32)
    rank_of = (slot % PAD).astype(jnp.float32)
    before = (
        lax.broadcasted_iota(jnp.int32, (tokens, tokens), 0)
        < lax.broadcasted_iota(jnp.int32, (tokens, tokens), 1)
    ).astype(jnp.bfloat16)

    def take(offset):
        block = x if offset == 0 else xs.at[offset]
        table = (info if offset == 0 else infos.at[offset])[...].astype(jnp.float32)
        named = jnp.zeros((slots, tokens), jnp.float32)
        weight = jnp.zeros((slots, tokens), jnp.float32)
        for k in range(TOP):
            same = (table[TOP + k : TOP + k + 1, :] == expert).astype(jnp.float32)
            named = named + same
            weight = weight + same * table[k : k + 1, :]
        rank = jnp.dot(named.astype(jnp.bfloat16), before, preferred_element_type=jnp.float32)
        chosen = jnp.where(rank == rank_of, named, 0.0)
        placed[offset] = chosen.astype(jnp.bfloat16)
        scale[offset] = jnp.sum(chosen * weight, axis=1, keepdims=True)
        rows[offset] = jnp.dot(
            chosen.astype(jnp.bfloat16), block[...], preferred_element_type=jnp.float32
        ).astype(jnp.bfloat16)

    take(0)
    for step in range(1, far + 1):
        for copies in sends:
            for copy in copies:
                copy.wait()
        if step < far:
            sends = [ring(step + 1, 0), ring(step + 1, 1)]
            for copies in sends:
                for copy in copies:
                    copy.start()
        else:
            for way in range(2):
                adapt_ring(1, way).start()
        take(step)
        if step < far:
            take(count - step)

    def one_expert(l):
        for which in range(2):
            own_weight(l, which).wait()
            sent_weight(l, which).wait()
        at = pl.ds(pl.multiple_of(l * PAD, PAD), PAD)
        taken = jnp.concatenate([rows[o, at, :] for o in range(count)], axis=0)
        product = lax.dot_general(
            taken[:, :half_width], wo[0, l], (((1,), (1,)), ((), ())), preferred_element_type=jnp.float32
        ) + lax.dot_general(
            taken[:, half_width:], wo[1, l], (((1,), (1,)), ((), ())), preferred_element_type=jnp.float32
        )
        for o in range(count):
            source = index_of((seat + count - o) % count, count)
            slope = silu_slope(pre[source, l].astype(jnp.float32))
            part = product[o * PAD : o * PAD + depth] * scale[o, at, :][:depth] * slope
            part = jnp.concatenate([part, jnp.zeros((PAD - depth, fw), jnp.float32)], axis=0)
            hidden[o * PAD : (o + 1) * PAD] = part.astype(jnp.bfloat16)
        for c in range(2):
            grads = lax.dot_general(
                hidden[...], wi[c, l], (((1,), (1,)), ((), ())), preferred_element_type=jnp.float32
            ).astype(jnp.bfloat16)
            for o in range(count):
                back[o, at, c * half_width : (c + 1) * half_width] = grads[o * PAD : (o + 1) * PAD]

    share = experts // far
    for step in range(1, far + 1):
        pl.loop(share * (step - 1), share * step if step < far else experts)(one_expert)
        for way in range(2):
            adapt_ring(step, way).wait()
        if step < far:
            for way in range(2):
                adapt_ring(step + 1, way).start()
        for offset in sorted({step, count - step}):
            adapt_twin(offset).start()
            adapt_sibling(offset, 0).start()

    def total(offset):
        return lax.dot_general(
            placed[offset], back[offset], (((0,), (0,)), ((), ())), preferred_element_type=jnp.float32
        )

    def hop(step, way):
        at = pl.ds(way * half, half) if step == 1 else pl.ds(0, tokens)
        return pltpu.make_async_remote_copy(
            outbox.at[way, step - 1, at], inbox.at[way, step - 1, at],
            r_send.at[way, step - 1], r_recv.at[way, step - 1],
            device_id=(right, left)[way], device_id_type=MESH,
        )

    outbox[0, 0] = total(far).astype(jnp.bfloat16)
    outbox[1, 0, half:] = outbox[0, 0, half:]
    hops = [hop(1, 0), hop(1, 1)]
    for copy in hops:
        copy.start()
    for step in range(2, far + 1):
        distance = far + 1 - step
        mine = [total(count - distance), total(distance)]
        later = []
        for way in range(2):
            hops[way].wait()
            if step == 2:
                at = slice(way * half, (way + 1) * half)
                rest = slice((1 - way) * half, (2 - way) * half)
                outbox[way, 1, at] = (
                    mine[way][at] + inbox[way, 0, at].astype(jnp.float32)
                ).astype(jnp.bfloat16)
                outbox[way, 1, rest] = mine[way][rest].astype(jnp.bfloat16)
            else:
                outbox[way, step - 1] = (
                    mine[way] + inbox[way, step - 2].astype(jnp.float32)
                ).astype(jnp.bfloat16)
            copy = hop(step, way)
            copy.start()
            later.append(copy)
        hops = later
        for offset in (step - 1, count - step + 1):
            adapt_twin(offset).wait()
            adapt_sibling(offset, 1).start()
    result = total(0)
    for way in range(2):
        hops[way].wait()
        result = result + inbox[way, far - 1].astype(jnp.float32)
    result = result.astype(jnp.bfloat16)
    token_out[...] = result

    vis = shuffled_out.shape[0]
    row = lax.broadcasted_iota(jnp.int32, (vis, tokens), 0)
    theirs = (slot_row[...] == row + (1 - core) * vis).astype(jnp.bfloat16)
    vis_send[...] = jnp.dot(theirs, result, preferred_element_type=jnp.float32).astype(jnp.bfloat16)
    copy = pltpu.make_async_remote_copy(
        vis_send, vis_recv, v_send, v_recv, device_id=sibling, device_id_type=MESH
    )
    copy.start()
    adapt_twin(far).wait()
    adapt_sibling(far, 1).start()
    ours = (slot_row[...] == row + core * vis).astype(jnp.bfloat16)
    kept = jnp.dot(ours, result, preferred_element_type=jnp.float32)
    copy.wait()
    visual = kept + vis_recv[...].astype(jnp.float32)
    adapter = (visual * slope_in[...]).astype(jnp.bfloat16)
    adapt_own.wait()
    for offset in range(count):
        for mine in range(2):
            adapt_sibling(offset, mine).wait()
    wide = 256
    for begin in range(0, wa.shape[0], wide):
        end = min(begin + wide, wa.shape[0])
        shuffled_out[:, begin:end] = lax.dot_general(
            adapter, wa[begin:end], (((1,), (1,)), ((), ())), preferred_element_type=jnp.float32
        )


def block_exchange(out_grad, gates, routes, tile_slot, w_in, w_out, expert_pre, adapter_pre, w_adapt):
    count = lax.axis_size("expert")
    tokens, width = out_grad.shape
    experts, fw, half_width = w_out.shape
    info = jnp.concatenate([gates.T, routes.T.astype(jnp.bfloat16)], axis=0)
    info = jnp.pad(info, ((0, PAD - 2 * TOP), (0, 0)))
    vis_count = adapter_pre.shape[0]
    outputs = w_adapt.shape[0] * count * 2
    slope = gelu_slope(adapter_pre.astype(jnp.float32))
    slots = experts * PAD
    bf16 = jnp.bfloat16
    dma = pltpu.SemaphoreType.DMA
    far = count // 2
    vmem = pl.BlockSpec(memory_space=pltpu.VMEM)
    return pl.pallas_call(
        exchange_kernel,
        out_shape=(
            jax.ShapeDtypeStruct((tokens, width), bf16),
            jax.ShapeDtypeStruct((vis_count, outputs), jnp.float32),
        ),
        in_specs=[vmem] * 5 + [pl.BlockSpec(memory_space=pl.ANY)] * 3,
        out_specs=(vmem, vmem),
        scratch_shapes=[
            pltpu.VMEM((count, tokens, width), bf16),
            pltpu.VMEM((count, PAD, tokens), bf16),
            pltpu.VMEM((2, experts, fw, half_width), bf16),
            pltpu.VMEM((2, experts, half_width, fw), bf16),
            pltpu.VMEM((count, slots, tokens), bf16),
            pltpu.VMEM((count, slots, width), bf16),
            pltpu.VMEM((count, slots, width), bf16),
            pltpu.VMEM((count, slots, 1), jnp.float32),
            pltpu.VMEM((count * PAD, fw), bf16),
            pltpu.VMEM((2, far, tokens, width), bf16),
            pltpu.VMEM((2, far, tokens, width), bf16),
            pltpu.VMEM((vis_count, width), bf16),
            pltpu.VMEM((vis_count, width), bf16),
            pltpu.VMEM((outputs, width), bf16),
            dma((2, far + 1)), dma((2, far + 1)), dma((2, far + 1)), dma((2, far + 1)),
            dma((2, experts)), dma((2, experts)), dma((2, experts)),
            dma((2, far)), dma((2, far)), dma, dma,
            dma, dma((2, far + 1)), dma((2, far + 1)), dma((count,)), dma((count,)), dma((2, count)), dma((2, count)),
        ],
        compiler_params=pltpu.CompilerParams(
            collective_id=0, has_side_effects=True, vmem_limit_bytes=61 << 20
        ),
        cost_estimate=pl.CostEstimate(
            flops=4 * experts * count * PAD * width * fw, bytes_accessed=4 * experts * width * fw, transcendentals=0
        ),
    )(out_grad, info, tile_slot.reshape(1, tokens), expert_pre, slope, w_out, w_in, w_adapt)


def body(out_grad, gates, routes, tile_slot, w_in, w_out, expert_pre, adapter_pre, w_adapt):
    vis_count = adapter_pre.shape[0]
    sizes = (lax.axis_size("groups"), lax.axis_size("expert"), lax.axis_size("dp"))
    if sizes == (2, 8, 2) and out_grad.shape[0] == 128 and expert_pre.shape[2] <= PAD:
        token_grads, shuffled = block_exchange(
            out_grad, gates, routes, tile_slot, w_in, w_out, expert_pre, adapter_pre, w_adapt
        )
    else:
        token_grads, visual_grad = row_exchange(
            out_grad, gates, routes, tile_slot, w_in, w_out, expert_pre, vis_count
        )
        adapter_grad = (visual_grad * gelu_slope(adapter_pre.astype(jnp.float32))).astype(jnp.bfloat16)
        shuffled = lax.dot_general(
            adapter_grad,
            lax.all_gather(w_adapt, ("expert", "dp"), axis=0, tiled=True),
            (((1,), (1,)), ((), ())),
            preferred_element_type=jnp.float32,
        )
    tile_cols = vis_count // TILE_R
    patch_grads = shuffled.reshape(TILE_R, tile_cols, 2, 2, SIGW).transpose(0, 2, 1, 3, 4)
    patch_grads = patch_grads.reshape(2 * TILE_R, 2 * tile_cols * SIGW)
    return (token_grads, patch_grads)


def solution(mesh):
    placed = (
        P(("groups", "expert", "dp"), None),
        P(("groups", "expert", "dp"), None),
        P(("groups", "expert", "dp"), None),
        P(("groups", "expert", "dp")),
        P("expert", "dp", None),
        P("expert", None, "dp"),
        P(("groups", "expert", "dp"), None, None, None),
        P(("groups", "expert", "dp"), None),
        P(("expert", "dp"), None),
    )
    return jax.shard_map(
        body,
        mesh=mesh,
        in_specs=placed,
        out_specs=(P(("groups", "expert", "dp"), None), P(("groups", "expert", "dp"), None)),
        check_vma=False,
    )
```

```python
import jax
import jax.numpy as jnp
from jax import lax
from jax.experimental import pallas as pl
from jax.experimental.pallas import tpu as pltpu
from jax.sharding import PartitionSpec as P

EXPERTS = 64
TOP = 6
SIGW = 576
TILE_R = 8


def silu_slope(value):
    sigma = jax.nn.sigmoid(value)
    return sigma * (1.0 + value * (1.0 - sigma))


def gelu_slope(value):
    normal_cdf = 0.5 * (1.0 + lax.erf(value * 0.7071067811865476))
    return normal_cdf + value * jnp.exp(-0.5 * value * value) * 0.3989422804014327


def row_exchange(out_grad, gates, routes, tile_slot, w_in, w_out, expert_pre, vis_count):
    axis_count = lax.axis_size("expert")
    core_count = lax.axis_size("dp")
    tok_count, feature_width = out_grad.shape
    top_count = routes.shape[1]
    local_experts = w_in.shape[0]
    replicas = max(1, axis_count // EXPERTS)
    slot_depth = expert_pre.shape[2]
    slot_total = axis_count * local_experts * slot_depth
    flat_routes = routes.reshape(-1)
    expert_hot = (flat_routes[:, None] == jnp.arange(EXPERTS, dtype=jnp.int32)[None, :]).astype(
        jnp.int32
    )
    earlier = jnp.cumsum(expert_hot, axis=0) - expert_hot
    row_rank = jnp.sum(earlier * expert_hot, axis=1)
    slot_range = jnp.arange(slot_total, dtype=jnp.int32)[None, :]
    row_hits = jnp.zeros((tok_count * top_count, slot_total), jnp.bool_)
    for piece in range(replicas):
        slot_id = (flat_routes + piece * EXPERTS) * slot_depth + row_rank
        row_hits = jnp.logical_or(row_hits, slot_id[:, None] == slot_range)
    token_slot = row_hits.reshape(tok_count, top_count, slot_total)
    placing = jnp.sum(token_slot.astype(jnp.bfloat16), axis=1)
    gate_slot = jnp.sum(
        jnp.where(token_slot, gates.astype(jnp.float32)[:, :, None], 0.0), axis=(0, 1)
    ).astype(jnp.bfloat16)
    send_rows = lax.dot_general(
        placing, out_grad, (((0,), (0,)), ((), ())), preferred_element_type=jnp.float32
    )
    send_rows = send_rows.astype(jnp.bfloat16).reshape(
        axis_count, local_experts, slot_depth, feature_width
    )
    gate_slot = gate_slot.reshape(axis_count, local_experts, slot_depth)
    recv_rows, recv_gates = (
        lax.all_to_all(send_rows, "expert", split_axis=0, concat_axis=0, tiled=True),
        lax.all_to_all(gate_slot, "expert", split_axis=0, concat_axis=0, tiled=True),
    )
    full_in, full_out = (
        lax.all_gather(w_in, "dp", axis=1, tiled=True),
        lax.all_gather(w_out, "dp", axis=2, tiled=True),
    )
    hidden_grad = jnp.einsum(
        "nlcd,lfd->nlcf", recv_rows, full_out, preferred_element_type=jnp.float32
    )
    hidden_grad = (
        hidden_grad
        * recv_gates.astype(jnp.float32)[..., None]
        * silu_slope(expert_pre.astype(jnp.float32))
    )
    hidden_grad = hidden_grad.astype(jnp.bfloat16)
    row_grad = jnp.einsum(
        "nlcf,ldf->nlcd", hidden_grad, full_in, preferred_element_type=jnp.float32
    ).astype(jnp.bfloat16)
    returned = lax.all_to_all(row_grad, "expert", split_axis=0, concat_axis=0, tiled=True)
    token_grads = jnp.dot(
        placing, returned.reshape(slot_total, feature_width), preferred_element_type=jnp.float32
    ).astype(jnp.bfloat16)
    owner_hot = (
        tile_slot[None, :] == jnp.arange(core_count * vis_count, dtype=jnp.int32)[:, None]
    ).astype(jnp.bfloat16)
    outgoing = jnp.dot(owner_hot, token_grads, preferred_element_type=jnp.float32).astype(
        jnp.bfloat16
    )
    incoming = lax.all_to_all(
        outgoing.reshape(core_count, vis_count, feature_width),
        "dp",
        split_axis=0,
        concat_axis=0,
        tiled=True,
    )
    return token_grads, jnp.sum(incoming.astype(jnp.float32), axis=0)


PAD = 16
MESH = pl.DeviceIdType.MESH


def seat_of(index, count):
    odd, half = index % 2, index // 2
    return half * (1 - odd) + (count - 1 - half) * odd


def index_of(seat, count):
    back = seat // (count // 2)
    return 2 * seat * (1 - back) + (2 * (count - 1 - seat) + 1) * back


def exchange_kernel(
    x, info, slot_row, pre, slope_in, w_out, w_in, w_adapt, token_out, patch_out,
    xs, infos, wo, wi, placed, rows, back, scale, hidden, outbox, inbox, vis_send, vis_recv, wa,
    x_send, x_recv, i_send, i_recv, w_local, w_send, w_recv, r_send, r_recv, v_send, v_recv,
    a_own, a_send, a_recv, y_send, y_recv, s_send, s_recv,
):
    count, tokens, width = xs.shape
    experts, fw, half_width = wo.shape[1], wo.shape[2], wo.shape[3]
    slots = experts * PAD
    depth = pre.shape[2]
    half = tokens // 2
    far = count // 2
    core = lax.axis_index("dp")
    expert_index = lax.axis_index("expert")
    seat = seat_of(expert_index, count)
    right = {"expert": index_of((seat + 1) % count, count)}
    left = {"expert": index_of((seat + count - 1) % count, count)}
    sibling = {"dp": 1 - core}
    group = lax.axis_index("groups")
    twin = {"groups": 1 - group}
    shard = w_adapt.shape[0]
    cut = (shard // 2 + PAD - 1) // PAD * PAD

    def columns(which):
        return pl.ds(pl.multiple_of(which * half_width, 128), half_width)

    def shard_at(offset, start=0, size=None):
        owner = index_of((seat + count - offset) % count, count)
        first = pl.multiple_of((owner * 2 + core) * shard + start, PAD)
        return pl.ds(first, shard if size is None else size)

    def adapt_ring(step, way):
        offset = step - 1 if way == 0 else (count - step + 1) % count
        start, size = (0, shard) if step < far else ((0, cut), (cut, shard - cut))[way]
        place = wa.at[shard_at(offset, start, size), columns(group)]
        source = w_adapt.at[pl.ds(start, size), columns(group)] if step == 1 else place
        return pltpu.make_async_remote_copy(
            source, place, a_send.at[way, step], a_recv.at[way, step],
            device_id=(right, left)[way], device_id_type=MESH,
        )

    def adapt_twin(offset):
        place = wa.at[shard_at(offset), columns(group)]
        return pltpu.make_async_remote_copy(
            place, place, y_send.at[offset], y_recv.at[offset], device_id=twin, device_id_type=MESH
        )

    def adapt_sibling(offset, mine):
        which = group if mine == 0 else 1 - group
        place = wa.at[shard_at(offset), columns(which)]
        source = w_adapt.at[:, columns(which)] if offset == 0 else place
        return pltpu.make_async_remote_copy(
            source, place, s_send.at[mine, offset], s_recv.at[mine, offset],
            device_id=sibling, device_id_type=MESH,
        )

    adapt_own = pltpu.make_async_copy(w_adapt, wa.at[shard_at(0)], a_own)

    def own_weight(l, which):
        source, target = ((w_out, wo), (w_in, wi))[which]
        return pltpu.make_async_copy(source.at[l], target.at[core, l], w_local.at[which, l])

    def sent_weight(l, which):
        source, target = ((w_out, wo), (w_in, wi))[which]
        return pltpu.make_async_remote_copy(
            source.at[l], target.at[core, l], w_send.at[which, l], w_recv.at[which, l],
            device_id=sibling, device_id_type=MESH,
        )

    barrier = pltpu.get_barrier_semaphore()
    for other in (left, right, sibling, twin):
        pl.semaphore_signal(barrier, inc=1, device_id=other, device_id_type=MESH)
    pl.semaphore_wait(barrier, 4)

    def ring(step, way):
        come, go = (step - 1, step) if way == 0 else ((count - step + 1) % count, count - step)
        block = x if step == 1 else xs.at[come]
        note = info if step == 1 else infos.at[come]
        to = (right, left)[way]
        copies = []
        at = pl.ds(way * half, half) if step == far else pl.ds(0, tokens)
        copies.append(
            pltpu.make_async_remote_copy(
                block.at[at], xs.at[go, at], x_send.at[way, step], x_recv.at[way, step],
                device_id=to, device_id_type=MESH,
            )
        )
        if step < far or way == 0:
            copies.append(
                pltpu.make_async_remote_copy(
                    note, infos.at[go], i_send.at[way, step], i_recv.at[way, step],
                    device_id=to, device_id_type=MESH,
                )
            )
        return copies

    sends = [ring(1, 0), ring(1, 1)]
    for copies in sends:
        for copy in copies:
            copy.start()

    @pl.loop(0, experts)
    def _(l):
        for which in range(2):
            sent_weight(l, which).start()
            own_weight(l, which).start()

    adapt_own.start()
    for mine in range(2):
        adapt_sibling(0, mine).start()

    slot = lax.broadcasted_iota(jnp.int32, (slots, tokens), 0)
    expert = (expert_index * experts + slot // PAD).astype(jnp.float32)
    rank_of = (slot % PAD).astype(jnp.float32)
    before = (
        lax.broadcasted_iota(jnp.int32, (tokens, tokens), 0)
        < lax.broadcasted_iota(jnp.int32, (tokens, tokens), 1)
    ).astype(jnp.bfloat16)

    def take(offset):
        block = x if offset == 0 else xs.at[offset]
        table = (info if offset == 0 else infos.at[offset])[...].astype(jnp.float32)
        named = jnp.zeros((slots, tokens), jnp.float32)
        weight = jnp.zeros((slots, tokens), jnp.float32)
        for k in range(TOP):
            same = (table[TOP + k : TOP + k + 1, :] == expert).astype(jnp.float32)
            named = named + same
            weight = weight + same * table[k : k + 1, :]
        rank = jnp.dot(named.astype(jnp.bfloat16), before, preferred_element_type=jnp.float32)
        chosen = jnp.where(rank == rank_of, named, 0.0)
        placed[offset] = chosen.astype(jnp.bfloat16)
        scale[offset] = jnp.sum(chosen * weight, axis=1, keepdims=True)
        rows[offset] = jnp.dot(
            chosen.astype(jnp.bfloat16), block[...], preferred_element_type=jnp.float32
        ).astype(jnp.bfloat16)

    take(0)
    for step in range(1, far + 1):
        for copies in sends:
            for copy in copies:
                copy.wait()
        if step < far:
            sends = [ring(step + 1, 0), ring(step + 1, 1)]
            for copies in sends:
                for copy in copies:
                    copy.start()
        else:
            for way in range(2):
                adapt_ring(1, way).start()
        take(step)
        if step < far:
            take(count - step)

    def one_expert(l):
        for which in range(2):
            own_weight(l, which).wait()
            sent_weight(l, which).wait()
        at = pl.ds(pl.multiple_of(l * PAD, PAD), PAD)
        taken = jnp.concatenate([rows[o, at, :] for o in range(count)], axis=0)
        product = lax.dot_general(
            taken[:, :half_width], wo[0, l], (((1,), (1,)), ((), ())), preferred_element_type=jnp.float32
        ) + lax.dot_general(
            taken[:, half_width:], wo[1, l], (((1,), (1,)), ((), ())), preferred_element_type=jnp.float32
        )
        for o in range(count):
            source = index_of((seat + count - o) % count, count)
            slope = silu_slope(pre[source, l].astype(jnp.float32))
            part = product[o * PAD : o * PAD + depth] * scale[o, at, :][:depth] * slope
            part = jnp.concatenate([part, jnp.zeros((PAD - depth, fw), jnp.float32)], axis=0)
            hidden[o * PAD : (o + 1) * PAD] = part.astype(jnp.bfloat16)
        for c in range(2):
            grads = lax.dot_general(
                hidden[...], wi[c, l], (((1,), (1,)), ((), ())), preferred_element_type=jnp.float32
            ).astype(jnp.bfloat16)
            for o in range(count):
                back[o, at, c * half_width : (c + 1) * half_width] = grads[o * PAD : (o + 1) * PAD]

    share = experts // far
    for step in range(1, far + 1):
        pl.loop(share * (step - 1), share * step if step < far else experts)(one_expert)
        for way in range(2):
            adapt_ring(step, way).wait()
        if step < far:
            for way in range(2):
                adapt_ring(step + 1, way).start()
        for offset in sorted({step, count - step}):
            adapt_twin(offset).start()
            adapt_sibling(offset, 0).start()

    def total(offset):
        return lax.dot_general(
            placed[offset], back[offset], (((0,), (0,)), ((), ())), preferred_element_type=jnp.float32
        )

    def hop(step, way):
        at = pl.ds(way * half, half) if step == 1 else pl.ds(0, tokens)
        return pltpu.make_async_remote_copy(
            outbox.at[way, step - 1, at], inbox.at[way, step - 1, at],
            r_send.at[way, step - 1], r_recv.at[way, step - 1],
            device_id=(right, left)[way], device_id_type=MESH,
        )

    outbox[0, 0] = total(far).astype(jnp.bfloat16)
    outbox[1, 0, half:] = outbox[0, 0, half:]
    hops = [hop(1, 0), hop(1, 1)]
    for copy in hops:
        copy.start()
    for step in range(2, far + 1):
        distance = far + 1 - step
        mine = [total(count - distance), total(distance)]
        later = []
        for way in range(2):
            hops[way].wait()
            if step == 2:
                at = slice(way * half, (way + 1) * half)
                rest = slice((1 - way) * half, (2 - way) * half)
                outbox[way, 1, at] = (
                    mine[way][at] + inbox[way, 0, at].astype(jnp.float32)
                ).astype(jnp.bfloat16)
                outbox[way, 1, rest] = mine[way][rest].astype(jnp.bfloat16)
            else:
                outbox[way, step - 1] = (
                    mine[way] + inbox[way, step - 2].astype(jnp.float32)
                ).astype(jnp.bfloat16)
            copy = hop(step, way)
            copy.start()
            later.append(copy)
        hops = later
        for offset in (step - 1, count - step + 1):
            adapt_twin(offset).wait()
            adapt_sibling(offset, 1).start()
    result = total(0)
    for way in range(2):
        hops[way].wait()
        result = result + inbox[way, far - 1].astype(jnp.float32)
    result = result.astype(jnp.bfloat16)
    token_out[...] = result

    vis = slope_in.shape[0]
    row = lax.broadcasted_iota(jnp.int32, (vis, tokens), 0)
    theirs = (slot_row[...] == row + (1 - core) * vis).astype(jnp.bfloat16)
    vis_send[...] = jnp.dot(theirs, result, preferred_element_type=jnp.float32).astype(jnp.bfloat16)
    copy = pltpu.make_async_remote_copy(
        vis_send, vis_recv, v_send, v_recv, device_id=sibling, device_id_type=MESH
    )
    copy.start()
    adapt_twin(far).wait()
    adapt_sibling(far, 1).start()
    ours = (slot_row[...] == row + core * vis).astype(jnp.bfloat16)
    kept = jnp.dot(ours, result, preferred_element_type=jnp.float32)
    copy.wait()
    visual = kept + vis_recv[...].astype(jnp.float32)
    adapter = (visual * slope_in[...]).astype(jnp.bfloat16)
    adapt_own.wait()
    for offset in range(count):
        for mine in range(2):
            adapt_sibling(offset, mine).wait()
    span = wa.shape[0] // 2
    wide = 384
    tile_cols = vis // TILE_R
    deep = 2 * TILE_R
    target = lax.broadcasted_iota(jnp.int32, (2 * vis, vis), 0)
    origin = lax.broadcasted_iota(jnp.int32, (2 * vis, vis), 1)
    spread = []
    for y in range(2):
        holds = (target % deep // 2 * tile_cols + target // deep == origin) & (target % 2 == y)
        spread.append(
            jnp.dot(
                holds.astype(jnp.float32).astype(jnp.bfloat16), adapter, preferred_element_type=jnp.float32
            ).astype(jnp.bfloat16)
        )
    for begin in range(0, span, wide):
        size = min(wide, span - begin)
        grads = sum(
            lax.dot_general(
                spread[y],
                wa[y * span + begin : y * span + begin + size],
                (((1,), (1,)), ((), ())),
                preferred_element_type=jnp.float32,
            )
            for y in range(2)
        )
        for b in range(tile_cols):
            patch_out[:, b * span + begin : b * span + begin + size] = grads[b * deep : (b + 1) * deep]


def block_exchange(out_grad, gates, routes, tile_slot, w_in, w_out, expert_pre, adapter_pre, w_adapt):
    count = lax.axis_size("expert")
    tokens, width = out_grad.shape
    experts, fw, half_width = w_out.shape
    info = jnp.concatenate([gates.T, routes.T.astype(jnp.bfloat16)], axis=0)
    info = jnp.pad(info, ((0, PAD - 2 * TOP), (0, 0)))
    vis_count = adapter_pre.shape[0]
    outputs = w_adapt.shape[0] * count * 2
    slope = gelu_slope(adapter_pre.astype(jnp.float32))
    slots = experts * PAD
    bf16 = jnp.bfloat16
    dma = pltpu.SemaphoreType.DMA
    far = count // 2
    vmem = pl.BlockSpec(memory_space=pltpu.VMEM)
    return pl.pallas_call(
        exchange_kernel,
        out_shape=(
            jax.ShapeDtypeStruct((tokens, width), bf16),
            jax.ShapeDtypeStruct((2 * TILE_R, vis_count // TILE_R * outputs // 2), jnp.float32),
        ),
        in_specs=[vmem] * 5 + [pl.BlockSpec(memory_space=pl.ANY)] * 3,
        out_specs=(vmem, vmem),
        scratch_shapes=[
            pltpu.VMEM((count, tokens, width), bf16),
            pltpu.VMEM((count, PAD, tokens), bf16),
            pltpu.VMEM((2, experts, fw, half_width), bf16),
            pltpu.VMEM((2, experts, half_width, fw), bf16),
            pltpu.VMEM((count, slots, tokens), bf16),
            pltpu.VMEM((count, slots, width), bf16),
            pltpu.VMEM((count, slots, width), bf16),
            pltpu.VMEM((count, slots, 1), jnp.float32),
            pltpu.VMEM((count * PAD, fw), bf16),
            pltpu.VMEM((2, far, tokens, width), bf16),
            pltpu.VMEM((2, far, tokens, width), bf16),
            pltpu.VMEM((vis_count, width), bf16),
            pltpu.VMEM((vis_count, width), bf16),
            pltpu.VMEM((outputs, width), bf16),
            dma((2, far + 1)), dma((2, far + 1)), dma((2, far + 1)), dma((2, far + 1)),
            dma((2, experts)), dma((2, experts)), dma((2, experts)),
            dma((2, far)), dma((2, far)), dma, dma,
            dma, dma((2, far + 1)), dma((2, far + 1)), dma((count,)), dma((count,)), dma((2, count)), dma((2, count)),
        ],
        compiler_params=pltpu.CompilerParams(
            collective_id=0, has_side_effects=True, vmem_limit_bytes=61 << 20
        ),
        cost_estimate=pl.CostEstimate(
            flops=4 * experts * count * PAD * width * fw, bytes_accessed=4 * experts * width * fw, transcendentals=0
        ),
    )(out_grad, info, tile_slot.reshape(1, tokens), expert_pre, slope, w_out, w_in, w_adapt)


def body(out_grad, gates, routes, tile_slot, w_in, w_out, expert_pre, adapter_pre, w_adapt):
    vis_count = adapter_pre.shape[0]
    sizes = (lax.axis_size("groups"), lax.axis_size("expert"), lax.axis_size("dp"))
    if sizes == (2, 8, 2) and out_grad.shape[0] == 128 and expert_pre.shape[2] <= PAD:
        return block_exchange(
            out_grad, gates, routes, tile_slot, w_in, w_out, expert_pre, adapter_pre, w_adapt
        )
    token_grads, visual_grad = row_exchange(
        out_grad, gates, routes, tile_slot, w_in, w_out, expert_pre, vis_count
    )
    adapter_grad = (visual_grad * gelu_slope(adapter_pre.astype(jnp.float32))).astype(jnp.bfloat16)
    shuffled = lax.dot_general(
        adapter_grad,
        lax.all_gather(w_adapt, ("expert", "dp"), axis=0, tiled=True),
        (((1,), (1,)), ((), ())),
        preferred_element_type=jnp.float32,
    )
    tile_cols = vis_count // TILE_R
    patch_grads = shuffled.reshape(TILE_R, tile_cols, 2, 2, SIGW).transpose(0, 2, 1, 3, 4)
    patch_grads = patch_grads.reshape(2 * TILE_R, 2 * tile_cols * SIGW)
    return (token_grads, patch_grads)


def solution(mesh):
    placed = (
        P(("groups", "expert", "dp"), None),
        P(("groups", "expert", "dp"), None),
        P(("groups", "expert", "dp"), None),
        P(("groups", "expert", "dp")),
        P("expert", "dp", None),
        P("expert", None, "dp"),
        P(("groups", "expert", "dp"), None, None, None),
        P(("groups", "expert", "dp"), None),
        P(("expert", "dp"), None),
    )
    return jax.shard_map(
        body,
        mesh=mesh,
        in_specs=placed,
        out_specs=(P(("groups", "expert", "dp"), None), P(("groups", "expert", "dp"), None)),
        check_vma=False,
    )
```

```python
import jax
import jax.numpy as jnp
from jax import lax
from jax.experimental import pallas as pl
from jax.experimental.pallas import tpu as pltpu
from jax.sharding import PartitionSpec as P

EXPERTS = 64
TOP = 6
SIGW = 576
TILE_R = 8


def silu_slope(value):
    sigma = jax.nn.sigmoid(value)
    return sigma * (1.0 + value * (1.0 - sigma))


def gelu_slope(value):
    normal_cdf = 0.5 * (1.0 + lax.erf(value * 0.7071067811865476))
    return normal_cdf + value * jnp.exp(-0.5 * value * value) * 0.3989422804014327


def row_exchange(out_grad, gates, routes, tile_slot, w_in, w_out, expert_pre, vis_count):
    axis_count = lax.axis_size("expert")
    core_count = lax.axis_size("dp")
    tok_count, feature_width = out_grad.shape
    top_count = routes.shape[1]
    local_experts = w_in.shape[0]
    replicas = max(1, axis_count // EXPERTS)
    slot_depth = expert_pre.shape[2]
    slot_total = axis_count * local_experts * slot_depth
    flat_routes = routes.reshape(-1)
    expert_hot = (flat_routes[:, None] == jnp.arange(EXPERTS, dtype=jnp.int32)[None, :]).astype(
        jnp.int32
    )
    earlier = jnp.cumsum(expert_hot, axis=0) - expert_hot
    row_rank = jnp.sum(earlier * expert_hot, axis=1)
    slot_range = jnp.arange(slot_total, dtype=jnp.int32)[None, :]
    row_hits = jnp.zeros((tok_count * top_count, slot_total), jnp.bool_)
    for piece in range(replicas):
        slot_id = (flat_routes + piece * EXPERTS) * slot_depth + row_rank
        row_hits = jnp.logical_or(row_hits, slot_id[:, None] == slot_range)
    token_slot = row_hits.reshape(tok_count, top_count, slot_total)
    placing = jnp.sum(token_slot.astype(jnp.bfloat16), axis=1)
    gate_slot = jnp.sum(
        jnp.where(token_slot, gates.astype(jnp.float32)[:, :, None], 0.0), axis=(0, 1)
    ).astype(jnp.bfloat16)
    send_rows = lax.dot_general(
        placing, out_grad, (((0,), (0,)), ((), ())), preferred_element_type=jnp.float32
    )
    send_rows = send_rows.astype(jnp.bfloat16).reshape(
        axis_count, local_experts, slot_depth, feature_width
    )
    gate_slot = gate_slot.reshape(axis_count, local_experts, slot_depth)
    recv_rows, recv_gates = (
        lax.all_to_all(send_rows, "expert", split_axis=0, concat_axis=0, tiled=True),
        lax.all_to_all(gate_slot, "expert", split_axis=0, concat_axis=0, tiled=True),
    )
    full_in, full_out = (
        lax.all_gather(w_in, "dp", axis=1, tiled=True),
        lax.all_gather(w_out, "dp", axis=2, tiled=True),
    )
    hidden_grad = jnp.einsum(
        "nlcd,lfd->nlcf", recv_rows, full_out, preferred_element_type=jnp.float32
    )
    hidden_grad = (
        hidden_grad
        * recv_gates.astype(jnp.float32)[..., None]
        * silu_slope(expert_pre.astype(jnp.float32))
    )
    hidden_grad = hidden_grad.astype(jnp.bfloat16)
    row_grad = jnp.einsum(
        "nlcf,ldf->nlcd", hidden_grad, full_in, preferred_element_type=jnp.float32
    ).astype(jnp.bfloat16)
    returned = lax.all_to_all(row_grad, "expert", split_axis=0, concat_axis=0, tiled=True)
    token_grads = jnp.dot(
        placing, returned.reshape(slot_total, feature_width), preferred_element_type=jnp.float32
    ).astype(jnp.bfloat16)
    owner_hot = (
        tile_slot[None, :] == jnp.arange(core_count * vis_count, dtype=jnp.int32)[:, None]
    ).astype(jnp.bfloat16)
    outgoing = jnp.dot(owner_hot, token_grads, preferred_element_type=jnp.float32).astype(
        jnp.bfloat16
    )
    incoming = lax.all_to_all(
        outgoing.reshape(core_count, vis_count, feature_width),
        "dp",
        split_axis=0,
        concat_axis=0,
        tiled=True,
    )
    return token_grads, jnp.sum(incoming.astype(jnp.float32), axis=0)


PAD = 16
MESH = pl.DeviceIdType.MESH


def seat_of(index, count):
    odd, half = index % 2, index // 2
    return half * (1 - odd) + (count - 1 - half) * odd


def index_of(seat, count):
    back = seat // (count // 2)
    return 2 * seat * (1 - back) + (2 * (count - 1 - seat) + 1) * back


def exchange_kernel(
    x, info, slot_row, pre, slope_in, w_out, w_in, w_adapt, token_out, patch_out,
    xs, infos, wo, wi, placed, rows, back, scale, hidden, outbox, inbox, vis_send, vis_recv, wa,
    x_send, x_recv, i_send, i_recv, w_local, w_send, w_recv, r_send, r_recv, v_send, v_recv,
    a_own, a_send, a_recv, y_send, y_recv, s_send, s_recv,
):
    count, tokens, width = xs.shape
    experts, fw, half_width = wo.shape[1], wo.shape[2], wo.shape[3]
    slots = experts * PAD
    depth = pre.shape[2]
    half = tokens // 2
    far = count // 2
    core = lax.axis_index("dp")
    expert_index = lax.axis_index("expert")
    seat = seat_of(expert_index, count)
    right = {"expert": index_of((seat + 1) % count, count)}
    left = {"expert": index_of((seat + count - 1) % count, count)}
    sibling = {"dp": 1 - core}
    group = lax.axis_index("groups")
    twin = {"groups": 1 - group}
    shard = w_adapt.shape[0]
    cut = (shard // 2 + PAD - 1) // PAD * PAD

    def columns(which):
        return pl.ds(pl.multiple_of(which * half_width, 128), half_width)

    def shard_at(offset, start=0, size=None):
        owner = index_of((seat + count - offset) % count, count)
        first = pl.multiple_of((owner * 2 + core) * shard + start, PAD)
        return pl.ds(first, shard if size is None else size)

    def adapt_ring(step, way):
        offset = step - 1 if way == 0 else (count - step + 1) % count
        start, size = (0, shard) if step < far else ((0, cut), (cut, shard - cut))[way]
        place = wa.at[shard_at(offset, start, size), columns(group)]
        source = w_adapt.at[pl.ds(start, size), columns(group)] if step == 1 else place
        return pltpu.make_async_remote_copy(
            source, place, a_send.at[way, step], a_recv.at[way, step],
            device_id=(right, left)[way], device_id_type=MESH,
        )

    def adapt_twin(offset):
        place = wa.at[shard_at(offset), columns(group)]
        return pltpu.make_async_remote_copy(
            place, place, y_send.at[offset], y_recv.at[offset], device_id=twin, device_id_type=MESH
        )

    def adapt_sibling(offset, mine):
        which = group if mine == 0 else 1 - group
        place = wa.at[shard_at(offset), columns(which)]
        source = w_adapt.at[:, columns(which)] if offset == 0 else place
        return pltpu.make_async_remote_copy(
            source, place, s_send.at[mine, offset], s_recv.at[mine, offset],
            device_id=sibling, device_id_type=MESH,
        )

    adapt_own = pltpu.make_async_copy(w_adapt, wa.at[shard_at(0)], a_own)

    def own_weight(l, which):
        source, target = ((w_out, wo), (w_in, wi))[which]
        return pltpu.make_async_copy(source.at[l], target.at[core, l], w_local.at[which, l])

    def sent_weight(l, which):
        source, target = ((w_out, wo), (w_in, wi))[which]
        return pltpu.make_async_remote_copy(
            source.at[l], target.at[core, l], w_send.at[which, l], w_recv.at[which, l],
            device_id=sibling, device_id_type=MESH,
        )

    barrier = pltpu.get_barrier_semaphore()
    for other in (left, right, sibling, twin):
        pl.semaphore_signal(barrier, inc=1, device_id=other, device_id_type=MESH)
    pl.semaphore_wait(barrier, 4)

    def ring(step, way):
        come, go = (step - 1, step) if way == 0 else ((count - step + 1) % count, count - step)
        block = x if step == 1 else xs.at[come]
        note = info if step == 1 else infos.at[come]
        to = (right, left)[way]
        copies = {}
        for part in (0, 1) if step < far else (way,):
            at = pl.ds(part * half, half)
            copies[part] = pltpu.make_async_remote_copy(
                block.at[at], xs.at[go, at], x_send.at[way, step, part], x_recv.at[way, step, part],
                device_id=to, device_id_type=MESH,
            )
        if step < far or way == 0:
            copies[2] = pltpu.make_async_remote_copy(
                note, infos.at[go], i_send.at[way, step], i_recv.at[way, step],
                device_id=to, device_id_type=MESH,
            )
        return copies

    sends = [ring(1, 0), ring(1, 1)]
    for copies in sends:
        for copy in copies.values():
            copy.start()

    @pl.loop(0, experts)
    def _(l):
        for which in range(2):
            sent_weight(l, which).start()
            own_weight(l, which).start()

    adapt_own.start()
    for mine in range(2):
        adapt_sibling(0, mine).start()

    slot = lax.broadcasted_iota(jnp.int32, (slots, tokens), 0)
    expert = (expert_index * experts + slot // PAD).astype(jnp.float32)
    rank_of = (slot % PAD).astype(jnp.float32)
    before = (
        lax.broadcasted_iota(jnp.int32, (tokens, tokens), 0)
        < lax.broadcasted_iota(jnp.int32, (tokens, tokens), 1)
    ).astype(jnp.bfloat16)

    def take(offset):
        block = x if offset == 0 else xs.at[offset]
        table = (info if offset == 0 else infos.at[offset])[...].astype(jnp.float32)
        named = jnp.zeros((slots, tokens), jnp.float32)
        weight = jnp.zeros((slots, tokens), jnp.float32)
        for k in range(TOP):
            same = (table[TOP + k : TOP + k + 1, :] == expert).astype(jnp.float32)
            named = named + same
            weight = weight + same * table[k : k + 1, :]
        rank = jnp.dot(named.astype(jnp.bfloat16), before, preferred_element_type=jnp.float32)
        chosen = jnp.where(rank == rank_of, named, 0.0)
        placed[offset] = chosen.astype(jnp.bfloat16)
        scale[offset] = jnp.sum(chosen * weight, axis=1, keepdims=True)
        rows[offset] = jnp.dot(
            chosen.astype(jnp.bfloat16), block[...], preferred_element_type=jnp.float32
        ).astype(jnp.bfloat16)

    take(0)
    for step in range(1, far + 1):
        later = [ring(step + 1, way) if step < far else {} for way in range(2)]
        for part in range(3):
            for way in range(2):
                if part in sends[way]:
                    sends[way][part].wait()
                if part in later[way]:
                    later[way][part].start()
        sends = later
        if step == far:
            for way in range(2):
                adapt_ring(1, way).start()
        take(step)
        if step < far:
            take(count - step)

    def one_expert(l):
        for which in range(2):
            own_weight(l, which).wait()
            sent_weight(l, which).wait()
        at = pl.ds(pl.multiple_of(l * PAD, PAD), PAD)
        taken = jnp.concatenate([rows[o, at, :] for o in range(count)], axis=0)
        product = lax.dot_general(
            taken[:, :half_width], wo[0, l], (((1,), (1,)), ((), ())), preferred_element_type=jnp.float32
        ) + lax.dot_general(
            taken[:, half_width:], wo[1, l], (((1,), (1,)), ((), ())), preferred_element_type=jnp.float32
        )
        for o in range(count):
            source = index_of((seat + count - o) % count, count)
            slope = silu_slope(pre[source, l].astype(jnp.float32))
            part = product[o * PAD : o * PAD + depth] * scale[o, at, :][:depth] * slope
            part = jnp.concatenate([part, jnp.zeros((PAD - depth, fw), jnp.float32)], axis=0)
            hidden[o * PAD : (o + 1) * PAD] = part.astype(jnp.bfloat16)
        for c in range(2):
            grads = lax.dot_general(
                hidden[...], wi[c, l], (((1,), (1,)), ((), ())), preferred_element_type=jnp.float32
            ).astype(jnp.bfloat16)
            for o in range(count):
                back[o, at, c * half_width : (c + 1) * half_width] = grads[o * PAD : (o + 1) * PAD]

    share = experts // far
    for step in range(1, far + 1):
        pl.loop(share * (step - 1), share * step if step < far else experts)(one_expert)
        for way in range(2):
            adapt_ring(step, way).wait()
        if step < far:
            for way in range(2):
                adapt_ring(step + 1, way).start()
        for offset in sorted({step, count - step}):
            adapt_twin(offset).start()
            adapt_sibling(offset, 0).start()

    def total(offset):
        return lax.dot_general(
            placed[offset], back[offset], (((0,), (0,)), ((), ())), preferred_element_type=jnp.float32
        )

    def hop(step, way):
        at = pl.ds(way * half, half) if step == 1 else pl.ds(0, tokens)
        return pltpu.make_async_remote_copy(
            outbox.at[way, step - 1, at], inbox.at[way, step - 1, at],
            r_send.at[way, step - 1], r_recv.at[way, step - 1],
            device_id=(right, left)[way], device_id_type=MESH,
        )

    outbox[0, 0] = total(far).astype(jnp.bfloat16)
    outbox[1, 0, half:] = outbox[0, 0, half:]
    hops = [hop(1, 0), hop(1, 1)]
    for copy in hops:
        copy.start()
    for step in range(2, far + 1):
        distance = far + 1 - step
        mine = [total(count - distance), total(distance)]
        later = []
        for way in range(2):
            hops[way].wait()
            if step == 2:
                at = slice(way * half, (way + 1) * half)
                rest = slice((1 - way) * half, (2 - way) * half)
                outbox[way, 1, at] = (
                    mine[way][at] + inbox[way, 0, at].astype(jnp.float32)
                ).astype(jnp.bfloat16)
                outbox[way, 1, rest] = mine[way][rest].astype(jnp.bfloat16)
            else:
                outbox[way, step - 1] = (
                    mine[way] + inbox[way, step - 2].astype(jnp.float32)
                ).astype(jnp.bfloat16)
            copy = hop(step, way)
            copy.start()
            later.append(copy)
        hops = later
        for offset in (step - 1, count - step + 1):
            adapt_twin(offset).wait()
            adapt_sibling(offset, 1).start()
    result = total(0)
    for way in range(2):
        hops[way].wait()
        result = result + inbox[way, far - 1].astype(jnp.float32)
    result = result.astype(jnp.bfloat16)
    token_out[...] = result

    vis = slope_in.shape[0]
    row = lax.broadcasted_iota(jnp.int32, (vis, tokens), 0)
    theirs = (slot_row[...] == row + (1 - core) * vis).astype(jnp.bfloat16)
    vis_send[...] = jnp.dot(theirs, result, preferred_element_type=jnp.float32).astype(jnp.bfloat16)
    copy = pltpu.make_async_remote_copy(
        vis_send, vis_recv, v_send, v_recv, device_id=sibling, device_id_type=MESH
    )
    copy.start()
    adapt_twin(far).wait()
    adapt_sibling(far, 1).start()
    ours = (slot_row[...] == row + core * vis).astype(jnp.bfloat16)
    kept = jnp.dot(ours, result, preferred_element_type=jnp.float32)
    copy.wait()
    visual = kept + vis_recv[...].astype(jnp.float32)
    adapter = (visual * slope_in[...]).astype(jnp.bfloat16)
    adapt_own.wait()
    for offset in range(count):
        for mine in range(2):
            adapt_sibling(offset, mine).wait()
    span = wa.shape[0] // 2
    wide = 384
    tile_cols = vis // TILE_R
    deep = 2 * TILE_R
    target = lax.broadcasted_iota(jnp.int32, (2 * vis, vis), 0)
    origin = lax.broadcasted_iota(jnp.int32, (2 * vis, vis), 1)
    spread = []
    for y in range(2):
        holds = (target % deep // 2 * tile_cols + target // deep == origin) & (target % 2 == y)
        spread.append(
            jnp.dot(
                holds.astype(jnp.float32).astype(jnp.bfloat16), adapter, preferred_element_type=jnp.float32
            ).astype(jnp.bfloat16)
        )
    for begin in range(0, span, wide):
        size = min(wide, span - begin)
        grads = sum(
            lax.dot_general(
                spread[y],
                wa[y * span + begin : y * span + begin + size],
                (((1,), (1,)), ((), ())),
                preferred_element_type=jnp.float32,
            )
            for y in range(2)
        )
        for b in range(tile_cols):
            patch_out[:, b * span + begin : b * span + begin + size] = grads[b * deep : (b + 1) * deep]


def block_exchange(out_grad, gates, routes, tile_slot, w_in, w_out, expert_pre, adapter_pre, w_adapt):
    count = lax.axis_size("expert")
    tokens, width = out_grad.shape
    experts, fw, half_width = w_out.shape
    info = jnp.concatenate([gates.T, routes.T.astype(jnp.bfloat16)], axis=0)
    info = jnp.pad(info, ((0, PAD - 2 * TOP), (0, 0)))
    vis_count = adapter_pre.shape[0]
    outputs = w_adapt.shape[0] * count * 2
    slope = gelu_slope(adapter_pre.astype(jnp.float32))
    slots = experts * PAD
    bf16 = jnp.bfloat16
    dma = pltpu.SemaphoreType.DMA
    far = count // 2
    vmem = pl.BlockSpec(memory_space=pltpu.VMEM)
    return pl.pallas_call(
        exchange_kernel,
        out_shape=(
            jax.ShapeDtypeStruct((tokens, width), bf16),
            jax.ShapeDtypeStruct((2 * TILE_R, vis_count // TILE_R * outputs // 2), jnp.float32),
        ),
        in_specs=[vmem] * 5 + [pl.BlockSpec(memory_space=pl.ANY)] * 3,
        out_specs=(vmem, vmem),
        scratch_shapes=[
            pltpu.VMEM((count, tokens, width), bf16),
            pltpu.VMEM((count, PAD, tokens), bf16),
            pltpu.VMEM((2, experts, fw, half_width), bf16),
            pltpu.VMEM((2, experts, half_width, fw), bf16),
            pltpu.VMEM((count, slots, tokens), bf16),
            pltpu.VMEM((count, slots, width), bf16),
            pltpu.VMEM((count, slots, width), bf16),
            pltpu.VMEM((count, slots, 1), jnp.float32),
            pltpu.VMEM((count * PAD, fw), bf16),
            pltpu.VMEM((2, far, tokens, width), bf16),
            pltpu.VMEM((2, far, tokens, width), bf16),
            pltpu.VMEM((vis_count, width), bf16),
            pltpu.VMEM((vis_count, width), bf16),
            pltpu.VMEM((outputs, width), bf16),
            dma((2, far + 1, 2)), dma((2, far + 1, 2)), dma((2, far + 1)), dma((2, far + 1)),
            dma((2, experts)), dma((2, experts)), dma((2, experts)),
            dma((2, far)), dma((2, far)), dma, dma,
            dma, dma((2, far + 1)), dma((2, far + 1)), dma((count,)), dma((count,)), dma((2, count)), dma((2, count)),
        ],
        compiler_params=pltpu.CompilerParams(
            collective_id=0, has_side_effects=True, vmem_limit_bytes=61 << 20
        ),
        cost_estimate=pl.CostEstimate(
            flops=4 * experts * count * PAD * width * fw, bytes_accessed=4 * experts * width * fw, transcendentals=0
        ),
    )(out_grad, info, tile_slot.reshape(1, tokens), expert_pre, slope, w_out, w_in, w_adapt)


def body(out_grad, gates, routes, tile_slot, w_in, w_out, expert_pre, adapter_pre, w_adapt):
    vis_count = adapter_pre.shape[0]
    sizes = (lax.axis_size("groups"), lax.axis_size("expert"), lax.axis_size("dp"))
    if sizes == (2, 8, 2) and out_grad.shape[0] == 128 and expert_pre.shape[2] <= PAD:
        return block_exchange(
            out_grad, gates, routes, tile_slot, w_in, w_out, expert_pre, adapter_pre, w_adapt
        )
    token_grads, visual_grad = row_exchange(
        out_grad, gates, routes, tile_slot, w_in, w_out, expert_pre, vis_count
    )
    adapter_grad = (visual_grad * gelu_slope(adapter_pre.astype(jnp.float32))).astype(jnp.bfloat16)
    shuffled = lax.dot_general(
        adapter_grad,
        lax.all_gather(w_adapt, ("expert", "dp"), axis=0, tiled=True),
        (((1,), (1,)), ((), ())),
        preferred_element_type=jnp.float32,
    )
    tile_cols = vis_count // TILE_R
    patch_grads = shuffled.reshape(TILE_R, tile_cols, 2, 2, SIGW).transpose(0, 2, 1, 3, 4)
    patch_grads = patch_grads.reshape(2 * TILE_R, 2 * tile_cols * SIGW)
    return (token_grads, patch_grads)


def solution(mesh):
    placed = (
        P(("groups", "expert", "dp"), None),
        P(("groups", "expert", "dp"), None),
        P(("groups", "expert", "dp"), None),
        P(("groups", "expert", "dp")),
        P("expert", "dp", None),
        P("expert", None, "dp"),
        P(("groups", "expert", "dp"), None, None, None),
        P(("groups", "expert", "dp"), None),
        P(("expert", "dp"), None),
    )
    return jax.shard_map(
        body,
        mesh=mesh,
        in_specs=placed,
        out_specs=(P(("groups", "expert", "dp"), None), P(("groups", "expert", "dp"), None)),
        check_vma=False,
    )
```
